512 devices in a mesh: gx: 32 (over x_hi, z), gy: 16 (over y, x_lo, core).
Axes of the slice: x: 4 (x_hi: 2, x_lo: 2; x = x_hi * 2 + x_lo), y: 4, z: 16, core: 2. Of those that a mesh axis runs over, the one named last changes fastest.
Arguments:
- basis: float32 [3, 524288, 128], P(None, ('gx', 'gy')), may hold values from -6 to 6
- sphere_box: int32 [524288], P(('gx', 'gy')), may hold values from 0 to 255
- sphere_type: int32 [524288], P(('gx', 'gy')), may hold values from 0 to 7
- near_offsets: int32 [9, 2], replicated, may hold values from -1 to 1, as said below
- near_mats: float32 [9, 128, 128], replicated, may hold values from -0.5 to 0.5
- up_mat: float32 [128, 128], replicated, may hold values from -0.03125 to 0.03125
- top_mat: float32 [128, 128], replicated, may hold values from -0.09375 to 0.09375
- tmats: float32 [8, 128, 128], replicated, may hold values from -0.125 to 0.125
- bloch_angle: float32 [2], replicated, may hold values from -3.140625 to 3.140625
Outputs:
- next_vector: float32 [524288, 128], P(('gx', 'gy'))
- hess_column: float32 [4], replicated
The draws below stay inside these ranges and needn't reach their ends.
Inputs may be any that keep to these rules, and one draw needn't show every extreme that they name: `near_offsets`: the rows are the nine offsets with both entries in -1, 0, 1, each once.
All inputs are finite; a program needn't handle non-finite values.
Results may differ from the reference program's by a relative error of at most 0.0003.
Values sent between devices are 32-bit elements; how exact they have to be, the bound alone decides.
A program may use at most 64 MiB of HBM per device.

```python
import jax
import jax.numpy as jnp
from jax import lax

COEF = 128
SD = 1024
LX = 16
LY = 16
KB = 3
NTYPE = 8
NOFF = 9
TY = 16
NBX = 512
NBY = 256
QX = 64
QY = 32
SPH = 524288


def draw_basis(key, part):
    key = jax.random.fold_in(key, 3)
    common_key = jax.random.fold_in(key, 11)
    own_key = jax.random.fold_in(key, 12)
    common = jnp.clip(jax.random.normal(common_key, (1, SPH, COEF), jnp.float32), -4.0, 4.0)
    own = jnp.clip(jax.random.normal(own_key, (KB, SPH, COEF), jnp.float32), -4.0, 4.0)
    return 0.6 * common + 0.8 * own


def draw_near_offsets(key, part):
    key = jax.random.fold_in(key, 5)
    order = jax.random.permutation(key, NOFF).astype(jnp.int32)
    return jnp.stack([order // 3 - 1, order % 3 - 1], axis=1).astype(jnp.int32)


def touch_ends(entries, key, low, top_value):
    longest = entries.shape.index(max(entries.shape))
    spots = []
    for shift in (0, 1):
        where = [jax.random.randint(jax.random.fold_in(key, axis), (), 0, length) for axis, length in enumerate(entries.shape)]
        where[longest] = (where[longest] + shift) % entries.shape[longest]
        spots.append(tuple(where))
    return entries.at[spots[0]].set(low).at[spots[1]].set(top_value)


def scatter_about(rng, dims, width, most, kind=jnp.bfloat16):
    drawn = width * jax.random.normal(rng, dims, jnp.float32)
    return jnp.clip(drawn, min=-most, max=most).astype(kind)


def setup_inputs(seed: int = 0) -> dict:
    arg_keys = jax.random.split(jax.random.key(seed), 10)
    basis = draw_basis(jax.random.fold_in(arg_keys[9], 71), 0)
    sphere_box = touch_ends(jax.random.randint(arg_keys[1], (SPH,), 0, LX * LY), jax.random.fold_in(arg_keys[1], 1), 0, (LX * LY) - 1).astype(jnp.int32)
    sphere_type = touch_ends(jax.random.randint(arg_keys[2], (SPH,), 0, NTYPE), jax.random.fold_in(arg_keys[2], 1), 0, NTYPE - 1).astype(jnp.int32)
    near_offsets = draw_near_offsets(jax.random.fold_in(arg_keys[9], 71), 0)
    near_mats = scatter_about(arg_keys[4], (NOFF, COEF, COEF), COEF ** -0.5, 0.5, jnp.float32)
    up_mat = scatter_about(arg_keys[5], (COEF, COEF), (COEF * SD // 4) ** -0.5, 0.03125, jnp.float32)
    top_mat = scatter_about(arg_keys[6], (COEF, COEF), (COEF * 32) ** -0.5, 0.09375, jnp.float32)
    tmats = scatter_about(arg_keys[7], (NTYPE, COEF, COEF), (COEF * 16) ** -0.5, 0.125, jnp.float32)
    bloch_angle = jnp.clip(jax.random.uniform(arg_keys[8], (2,), jnp.float32, -3.140625, 3.140625), -3.140625, 3.140625)
    return {"basis": basis, "sphere_box": sphere_box, "sphere_type": sphere_type, "near_offsets": near_offsets, "near_mats": near_mats, "up_mat": up_mat, "top_mat": top_mat, "tmats": tmats, "bloch_angle": bloch_angle}


HIGHEST = lax.Precision.HIGHEST
wave_number = 2.3

def product(left, right):
    return jnp.dot(left, right, precision=HIGHEST, preferred_element_type=jnp.float32)

def rotate_pairs(values, angle):
    half_size = values.shape[-1] // 2
    real_part = values[..., :half_size]
    imag_part = values[..., half_size:]
    cosine = jnp.cos(angle)[..., None]
    sine_part = jnp.sin(angle)[..., None]
    return jnp.concatenate([cosine * real_part - sine_part * imag_part, sine_part * real_part + cosine * imag_part], axis=-1)

def far_weights(target_x, target_y, source_x, source_y, grid_x, grid_y, bloch_angle):
    shift_x = (source_x[None, :] - target_x[:, None] + grid_x // 2) % grid_x - grid_x // 2
    shift_y = (source_y[None, :] - target_y[:, None] + grid_y // 2) % grid_y - grid_y // 2
    cross_x = (target_x[:, None] + shift_x - source_x[None, :]) // grid_x
    cross_y = (target_y[:, None] + shift_y - source_y[None, :]) // grid_y
    reach = jnp.maximum(jnp.abs(shift_x), jnp.abs(shift_y))
    distance = (shift_x * shift_x + shift_y * shift_y).astype(jnp.float32)
    radius = jnp.sqrt(jnp.maximum(distance, 1.0))
    weight = jnp.where(reach >= 2, 16.0 / radius, 0.0)
    angle = wave_number * radius + cross_x.astype(jnp.float32) * bloch_angle[0] + cross_y.astype(jnp.float32) * bloch_angle[1]
    return (weight * jnp.cos(angle), weight * jnp.sin(angle))

def complex_apply(far_cos, far_sin, sources):
    half_size = sources.shape[1] // 2
    real_in = sources[:, :half_size]
    imag_in = sources[:, half_size:]
    real_out = product(far_cos, real_in) - product(far_sin, imag_in)
    imag_out = product(far_sin, real_in) + product(far_cos, imag_in)
    return jnp.concatenate([real_out, imag_out], axis=1)

def reference(basis, sphere_box, sphere_type, near_offsets, near_mats, up_mat, top_mat, tmats, bloch_angle):
    vector = basis[KB - 1]
    sphere_index = jnp.arange(SPH, dtype=jnp.int32)
    tile_index = sphere_index // SD
    box_row = tile_index // TY * LX + sphere_box // LY
    box_col = tile_index % TY * LY + sphere_box % LY
    flat_box = (box_row * NBY + box_col).astype(jnp.int32)
    leaf_mult = jax.ops.segment_sum(vector, flat_box, num_segments=NBX * NBY).reshape(NBX, NBY, COEF)
    padded = jnp.pad(leaf_mult, ((1, 1), (1, 1), (0, 0)), mode='wrap')
    rim_rows = jnp.arange(NBX + 2, dtype=jnp.int32)
    rim_cols = jnp.arange(NBY + 2, dtype=jnp.int32)
    cross_rows = jnp.where(rim_rows == 0, -1.0, 0.0) + jnp.where(rim_rows == NBX + 1, 1.0, 0.0)
    cross_cols = jnp.where(rim_cols == 0, -1.0, 0.0) + jnp.where(rim_cols == NBY + 1, 1.0, 0.0)
    padded = rotate_pairs(padded, cross_rows[:, None] * bloch_angle[0] + cross_cols[None, :] * bloch_angle[1])
    near = jnp.zeros((NBX * NBY, COEF), jnp.float32)
    start_zero = jnp.zeros((), jnp.int32)
    for entry in range(NOFF):
        window = lax.dynamic_slice(padded, (1 + near_offsets[entry, 0], 1 + near_offsets[entry, 1], start_zero), (NBX, NBY, COEF))
        near = near + product(window.reshape(NBX * NBY, COEF), near_mats[entry])
    quad_sum = leaf_mult.reshape(QX, LX // 2, QY, LY // 2, COEF).sum(axis=(1, 3)).reshape(QX * QY, COEF)
    expansion = product(quad_sum, up_mat)
    quad_index = jnp.arange(QX * QY, dtype=jnp.int32)
    quad_x = quad_index // QY
    quad_y = quad_index % QY
    far_cos, far_sin = far_weights(quad_x, quad_y, quad_x, quad_y, QX, QY, bloch_angle)
    far = complex_apply(far_cos, far_sin, expansion)
    far_top = product(far, top_mat)
    local_field = (near.reshape(QX, LX // 2, QY, LY // 2, COEF) + far_top.reshape(QX, 1, QY, 1, COEF)).reshape(NBX * NBY, COEF)
    field = local_field[flat_box]

    def apply_block(block):
        block_field, block_type = block
        chosen = tmats[block_type]
        return jnp.einsum('sk,skl->sl', block_field, chosen, precision=HIGHEST)
    scattered = lax.map(apply_block, (field.reshape(SPH // SD, SD, COEF), sphere_type.reshape(SPH // SD, SD))).reshape(SPH, COEF)
    image = vector - scattered
    count = SPH * COEF
    coeffs = jnp.einsum('ksc,sc->k', basis, image, precision=HIGHEST) / count
    reduced = image - jnp.einsum('k,ksc->sc', coeffs, basis, precision=HIGHEST)
    beta = jnp.sqrt(jnp.sum(reduced * reduced) / count + 1e-06)
    return (reduced / beta, jnp.concatenate([coeffs, beta[None]]))
```

```python
import functools

import jax
import jax.numpy as jnp
from jax import lax
from jax.experimental import pallas as pl
from jax.experimental.pallas import tpu as pltpu
from jax.sharding import PartitionSpec as P

SD = 1024
LX = 16
LY = 16
KB = 3
COEF = 128
NTYPE = 8
NOFF = 9
BOXES = LX * LY
CHUNK = 256

MESH = pl.DeviceIdType.MESH
wave_number = 2.3
f32 = jnp.float32
bf16 = jnp.bfloat16
i32 = jnp.int32


def iota(shape, dim):
    return lax.broadcasted_iota(i32, shape, dim)


def split(x):
    high = x.astype(bf16)
    return high, (x - high.astype(f32)).astype(bf16)


def dot(a, b):
    return jnp.dot(a, b, preferred_element_type=f32)


def ones_where(mask):
    return jnp.where(mask, 1.0, 0.0).astype(bf16)


def times_i(x):
    turned = pltpu.roll(x, COEF // 2, x.ndim - 1)
    return jnp.where(iota(x.shape, x.ndim - 1) < COEF // 2, -turned, turned)


def total_lane(x, lane):
    return jnp.sum(jnp.where(iota(x.shape, 1) == lane, x, 0.0), axis=1, keepdims=True)


def to_lanes(parts):
    rows = [jnp.sum(p, axis=0, keepdims=True) for p in parts]
    rows += [jnp.zeros((8 - len(rows), COEF), f32)]
    sums = jnp.sum(jnp.concatenate(rows, axis=0), axis=1, keepdims=True)
    placed = jnp.where(iota((8, COEF), 0) == iota((8, COEF), 1), sums, 0.0)
    return jnp.sum(placed, axis=0, keepdims=True)


def fold(x):
    return jnp.sum(x.reshape(x.shape[0] // 8, 8, COEF), axis=0)


def far_weights(nx, ny, gx, gy, theta):
    shape = (4 * ny, 8 * nx)
    m, n = iota(shape, 0), iota(shape, 1)
    grid_x, grid_y = 2 * nx, 2 * ny
    target_x, target_y = 2 * gx + ((m >> 1) & 1), 2 * (m >> 2) + (m & 1)
    source_x, source_y = 2 * (n >> 3) + ((n >> 1) & 1), 2 * gy + (n & 1)
    shift_x = ((source_x - target_x + grid_x // 2) & (grid_x - 1)) - grid_x // 2
    shift_y = ((source_y - target_y + grid_y // 2) & (grid_y - 1)) - grid_y // 2
    wraps_x, wraps_y = target_x + shift_x - source_x, target_y + shift_y - source_y
    cross_x = jnp.where(wraps_x > 0, 1.0, jnp.where(wraps_x < 0, -1.0, 0.0))
    cross_y = jnp.where(wraps_y > 0, 1.0, jnp.where(wraps_y < 0, -1.0, 0.0))
    reach = jnp.maximum(jnp.abs(shift_x), jnp.abs(shift_y))
    distance = (shift_x * shift_x + shift_y * shift_y).astype(f32)
    radius = jnp.sqrt(jnp.maximum(distance, 1.0))
    weight = jnp.where(reach >= 2, 16.0 / radius, 0.0)
    angle = wave_number * radius + cross_x * theta[0] + cross_y * theta[1]
    return weight * jnp.where((n & 4) == 0, jnp.cos(angle), jnp.sin(angle))


def kernel(
    nx, ny,
    basis_in, box_in, type_in, offsets_in, near_in, up_in, top_in, tmats_in, bloch_in,
    out_ref, hess_ref,
    basis, box, kind, offsets, near_mats, up, top, tmats, bloch,
    ebuf, gbuf, pbuf, rbuf, abuf, bbuf,
    edges, corners, rim, rim_corners, pad, far_w, top_t, hot, member_t, image, field,
    load_sem, e_sem, g_sem, r_sem, a_sem, b_sem, h_send, h_recv, out_sem,
):
    gx, gy = lax.axis_index("gx"), lax.axis_index("gy")
    count = float(nx * ny * SD * COEF)

    def load(src, dst, i):
        copy = pltpu.make_async_copy(src, dst, load_sem.at[i])
        copy.start()
        return copy

    load_vec = load(basis_in.at[KB - 1], basis.at[KB - 1], 0)
    load_box = load(box_in, box, 1)
    load_up = load(up_in, up, 2)
    load_bloch = load(bloch_in, bloch, 3)
    load_basis = load(basis_in.at[pl.ds(0, KB - 1)], basis.at[pl.ds(0, KB - 1)], 4)
    load_type = load(type_in, kind, 5)
    load_offsets = load(offsets_in, offsets, 6)
    load_near = load(near_in, near_mats, 7)
    load_top = load(top_in, top, 8)
    load_tmats = load(tmats_in, tmats, 9)

    barrier = pltpu.get_barrier_semaphore()

    def greet_x(k, c):
        pl.semaphore_signal(barrier, inc=1, device_id={"gx": (gx + k) % nx}, device_id_type=MESH)
        return c

    def greet_y(k, c):
        pl.semaphore_signal(barrier, inc=1, device_id={"gy": (gy + k) % ny}, device_id_type=MESH)
        return c

    lax.fori_loop(1, nx, greet_x, 0)
    lax.fori_loop(1, ny, greet_y, 0)
    sides = [(-1, 0), (1, 0), (0, -1), (0, 1), (-1, -1), (-1, 1), (1, -1), (1, 1)]

    def beside(side):
        return {"gx": (gx + side[0] + nx) % nx, "gy": (gy + side[1] + ny) % ny}

    for side in sides[4:]:
        pl.semaphore_signal(barrier, inc=1, device_id=beside(side), device_id_type=MESH)

    def send_x(buf, sem, rows):
        def body(k, c):
            near_half = nx // 2 + ((k + 1) // 2) * (1 - 2 * (k % 2))
            peer = (gx + near_half) % nx
            spot = buf.at[gx, pl.ds(0, rows)]
            pltpu.make_async_remote_copy(
                spot, spot, sem.at[0], sem.at[1], device_id={"gx": peer}, device_id_type=MESH
            ).start()
            return c

        lax.fori_loop(0, nx - 1, body, 0)

    def send_y(src, dst, sem, rows, scatter):
        def body(k, c):
            peer = (gy + k) % ny
            pltpu.make_async_remote_copy(
                src.at[peer if scatter else gy, pl.ds(0, rows)],
                dst.at[gy, pl.ds(0, rows)],
                sem.at[0], sem.at[1], device_id={"gy": peer}, device_id_type=MESH,
            ).start()
            return c

        lax.fori_loop(1, ny, body, 0)

    def wait_all(buf, sem, number, rows):
        span = buf.at[pl.ds(0, number), pl.ds(0, rows)]
        pltpu.make_async_copy(span, span, sem).wait()

    load_box.wait()
    boxes = box[...]
    member = jnp.concatenate(
        [ones_where(iota((BOXES, COEF), 0) == boxes[r : r + 1, :]) for r in range(SD // COEF)], axis=1
    )
    load_vec.wait()
    leaf2 = dot(member, jnp.concatenate(split(basis[KB - 1]), axis=1))
    leaf = (leaf2[:, :COEF] + leaf2[:, COEF:]).reshape(LX, LY, COEF)

    quads = []
    for a in range(2):
        for b in range(2):
            part = jnp.sum(leaf[a * 8 : a * 8 + 8, b * 8 : b * 8 + 8, :], axis=0)
            quads.append(jnp.sum(part, axis=0, keepdims=True))
    quad_sum = jnp.concatenate(quads + [jnp.zeros((4, COEF), f32)], axis=0)
    load_up.wait()
    quad_high, quad_low = split(quad_sum)
    pair = jnp.concatenate([quad_high.astype(f32), quad_low.astype(f32)], axis=0).astype(bf16)
    up_high, up_low = split(up[...])
    raised = dot(pair, up_high) + dot(pair, up_low)
    ebuf[gx, 0:4, :] = (raised[0:8] + raised[8:16])[0:4]
    pl.semaphore_wait(barrier, nx + ny + 2)
    send_x(ebuf, e_sem, 4)

    edges[0] = leaf[0]
    edges[1] = leaf[LX - 1]
    edges[2] = leaf[:, 0, :]
    edges[3] = leaf[:, LY - 1, :]
    for c, (x, y) in enumerate([(0, 0), (0, LY - 1), (LX - 1, 0), (LX - 1, LY - 1)]):
        corners[c, 0:1, :] = leaf[x, y : y + 1, :]
    halo = []
    for i, side in enumerate(sides):
        other = sides.index((-side[0], -side[1]))
        if i < 4:
            src, dst = edges.at[i], rim.at[other]
        else:
            src, dst = corners.at[i - 4], rim_corners.at[other - 4]
        copy = pltpu.make_async_remote_copy(
            src, dst, h_send.at[i], h_recv.at[other], device_id=beside(side), device_id_type=MESH
        )
        copy.start()
        halo.append(copy)
    pad[1 : LX + 1, 8 : 8 + LY, :] = leaf

    load_basis.wait()
    grams = []
    for j in range(KB):
        for k in range(j, KB):
            grams.append(fold(basis[j] * basis[k]))
    gbuf[gx, 0:1, :] = to_lanes(grams)
    send_x(gbuf, g_sem, 1)

    load_bloch.wait()
    theta = (bloch[0], bloch[1])
    weights = far_weights(nx, ny, gx, gy, theta)
    far_w[0], far_w[1] = split(weights)

    load_type.wait()
    codes = boxes + BOXES * kind[...]
    for r in range(SD // COEF):
        code = jnp.broadcast_to(codes[r : r + 1, :], (COEF, COEF)).T
        own_box = code & (BOXES - 1)
        own_type = code >> 8
        lane = iota((COEF, COEF), 1)
        rows = pl.ds(r * COEF, COEF)
        member_t[rows, 0:COEF] = ones_where(own_box == lane)
        member_t[rows, COEF:BOXES] = ones_where(own_box == lane + COEF)
        spot = own_type * 8 + ((own_box >> 7) & 1) * 2 + ((own_box >> 3) & 1)
        hot[rows, :] = ones_where(spot == (lane & 63))
        field[rows, :] = own_type

    load_top.wait()
    load_tmats.wait()
    every = jnp.concatenate([tmats[t] for t in range(NTYPE)], axis=1)
    every_high, every_low = split(every)
    top_high, top_low = split(top[...])
    top_t[0], top_t[1] = split(dot(top_high, every_high) + dot(top_low, every_high) + dot(top_high, every_low))
    every3 = jnp.concatenate([every_high, every_high, every_low], axis=0)

    load_offsets.wait()
    load_near.wait()
    for copy in halo:
        copy.wait_recv()
    crossings = []
    row_cross = {-1: jnp.where(gx == 0, -1.0, 0.0), 0: 0.0, 1: jnp.where(gx == nx - 1, 1.0, 0.0)}
    col_cross = {-1: jnp.where(gy == 0, -1.0, 0.0), 0: 0.0, 1: jnp.where(gy == ny - 1, 1.0, 0.0)}
    angle = jnp.zeros((8, COEF), f32)
    for i, side in enumerate(sides):
        value = row_cross[side[0]] * theta[0] + col_cross[side[1]] * theta[1]
        angle = jnp.where(iota((8, COEF), 0) == i, value, angle)
    cosine, sine = jnp.cos(angle), jnp.sin(angle)

    def rotated(x, i):
        return cosine[i : i + 1] * x + sine[i : i + 1] * times_i(x)

    pad[0, 8 : 8 + LY, :] = rotated(rim[0], 0)
    pad[LX + 1, 8 : 8 + LY, :] = rotated(rim[1], 1)
    west, east = rotated(rim[2], 2), rotated(rim[3], 3)
    for x in range(LX):
        pad[x + 1, 7:8, :] = west[x : x + 1, :]
        pad[x + 1, 8 + LY : 9 + LY, :] = east[x : x + 1, :]
    for c, (x, y) in enumerate([(0, 7), (0, 8 + LY), (LX + 1, 7), (LX + 1, 8 + LY)]):
        pad[x, y : y + 1, :] = rotated(rim_corners[c], 4 + c)

    highs, lows, mats_high, mats_low = [], [], [], []
    for b in (-1, 0, 1):
        shifted = pad[:, 8 + b : 8 + b + LY, :].reshape((LX + 2) * LY, COEF)
        high, low = split(shifted)
        for a in (-1, 0, 1):
            entry = 0
            for o in range(NOFF):
                here = (offsets[o, 0] == a) & (offsets[o, 1] == b)
                entry = jnp.where(here, o, entry)
            mat_high, mat_low = split(near_mats[entry])
            start = (1 + a) * LY
            highs.append(high[start : start + BOXES])
            lows.append(low[start : start + BOXES])
            mats_high.append(mat_high)
            mats_low.append(mat_low)
    mat_high = jnp.concatenate(mats_high, axis=0)
    mats = jnp.concatenate([mat_high, jnp.concatenate(mats_low, axis=0)], axis=1)
    near2 = dot(jnp.concatenate(highs, axis=1), mats)
    near = near2[:, :COEF] + near2[:, COEF:] + dot(jnp.concatenate(lows, axis=1), mat_high)

    wait_all(ebuf, e_sem.at[1], nx - 1, 4)
    sources = ebuf[...].reshape(8 * nx, COEF)
    turned = pltpu.roll(times_i(sources), 4, 0)
    sources = jnp.where((iota(sources.shape, 0) & 4) == 0, sources, turned)
    source_high, source_low = split(sources)
    part2 = dot(far_w[0], jnp.concatenate([source_high, source_low], axis=1))
    part = part2[:, :COEF] + part2[:, COEF:] + dot(far_w[1], source_high)
    wait_all(gbuf, g_sem.at[1], nx - 1, 1)
    gram_column = jnp.sum(gbuf[...], axis=0)
    for j in range(ny):
        pbuf[j, 0:4, :] = part[4 * j : 4 * j + 4]
        pbuf[j, 4:5, :] = gram_column
    rbuf[gy, 0:5, :] = pbuf[gy, 0:5, :]
    send_y(pbuf, rbuf, r_sem, 5, True)

    near_pair = jnp.concatenate(split(near), axis=1)
    for r in range(SD // CHUNK):
        rows = pl.ds(r * CHUNK, CHUNK)
        at2 = dot(member_t[rows, :], near_pair)
        at_high, at_low = split(at2[:, :COEF] + at2[:, COEF:])
        all_types = dot(jnp.concatenate([at_high, at_low, at_high], axis=1), every3)
        own_type = field[rows, :]
        value = all_types[:, :COEF]
        for t in range(1, NTYPE):
            value = jnp.where(own_type == t, all_types[:, t * COEF : (t + 1) * COEF], value)
        image[rows, :] = basis[KB - 1, rows, :] - value

    wait_all(rbuf, r_sem.at[1], ny - 1, 5)
    arrived = jnp.sum(rbuf[...], axis=0)
    far = jnp.where(iota((8, COEF), 0) < 4, arrived, 0.0)
    gram_row = arrived[4:5, :]
    far_high, far_low = split(far)
    far_pair = jnp.concatenate([far_high.astype(f32), far_low.astype(f32)], axis=0).astype(bf16)
    table2 = dot(far_pair, top_t[0]) + dot(far_pair, top_t[1])
    table = table2[0:8] + table2[8:16]
    table = jnp.concatenate([table[:, t * COEF : (t + 1) * COEF] for t in range(NTYPE)], axis=0)
    table = jnp.concatenate(split(table), axis=0)

    gram, lane = {}, 0
    for j in range(KB):
        for k in range(j, KB):
            gram[j, k] = gram[k, j] = total_lane(gram_row, lane)
            lane += 1
    guess = [gram[k, KB - 1] / count for k in range(KB)]
    sums = [jnp.zeros((8, COEF), f32)] * (KB + 1)
    for r in range(SD // CHUNK):
        rows = pl.ds(r * CHUNK, CHUNK)
        w = image[rows, :] - dot(hot[rows, :], table)
        vectors = [basis[k, rows, :] for k in range(KB)]
        for k in range(KB):
            w = w - guess[k] * vectors[k]
        image[rows, :] = w
        for k in range(KB):
            sums[k] = sums[k] + fold(vectors[k] * w)
        sums[KB] = sums[KB] + fold(w * w)

    abuf[gx, 0:1, :] = to_lanes(sums)
    send_x(abuf, a_sem, 1)
    wait_all(abuf, a_sem.at[1], nx - 1, 1)
    bbuf[gy, 0:1, :] = jnp.sum(abuf[...], axis=0)
    send_y(bbuf, bbuf, b_sem, 1, False)
    wait_all(bbuf, b_sem.at[1], ny - 1, 1)
    totals = jnp.sum(bbuf[...], axis=0)
    inner = [total_lane(totals, k) for k in range(KB)]
    square = total_lane(totals, KB)
    coeffs = []
    for k in range(KB):
        value = inner[k]
        for j in range(KB):
            value = value + gram[k, j] * guess[j]
        coeffs.append(value / count)
    step = [coeffs[k] - guess[k] for k in range(KB)]
    for k in range(KB):
        along = -2.0 * inner[k]
        for j in range(KB):
            along = along + gram[k, j] * step[j]
        square = square + step[k] * along
    beta = jnp.sqrt(jnp.maximum(square, 0.0) / count + 1e-06)
    scale = 1.0 / beta

    outs = []
    for r in range(SD // CHUNK):
        rows = pl.ds(r * CHUNK, CHUNK)
        w = image[rows, :]
        for k in range(KB):
            w = w - step[k] * basis[k, rows, :]
        image[rows, :] = w * scale
        copy = pltpu.make_async_copy(image.at[rows], out_ref.at[rows], out_sem.at[r])
        copy.start()
        outs.append(copy)
    for k, value in enumerate(coeffs + [beta]):
        hess_ref[k] = jnp.sum(value)
    for copy in halo:
        copy.wait_send()
    wait_all(ebuf, e_sem.at[0], nx - 1, 4)
    wait_all(gbuf, g_sem.at[0], nx - 1, 1)
    wait_all(pbuf, r_sem.at[0], ny - 1, 5)
    wait_all(abuf, a_sem.at[0], nx - 1, 1)
    wait_all(bbuf, b_sem.at[0], ny - 1, 1)
    for copy in outs:
        copy.wait()


def on_device(nx, ny, basis, sphere_box, sphere_type, near_offsets, near_mats, up_mat, top_mat, tmats, bloch_angle):
    vmem, dma = pltpu.VMEM, pltpu.SemaphoreType.DMA
    return pl.pallas_call(
        functools.partial(kernel, nx, ny),
        out_shape=(jax.ShapeDtypeStruct((SD, COEF), f32), jax.ShapeDtypeStruct((KB + 1,), f32)),
        in_specs=[pl.BlockSpec(memory_space=pl.ANY)] * 9,
        out_specs=(pl.BlockSpec(memory_space=pl.ANY), pl.BlockSpec(memory_space=pltpu.SMEM)),
        scratch_shapes=[
            vmem((KB, SD, COEF), f32),
            vmem((SD // COEF, COEF), i32),
            vmem((SD // COEF, COEF), i32),
            pltpu.SMEM((NOFF, 2), i32),
            vmem((NOFF, COEF, COEF), f32),
            vmem((COEF, COEF), f32),
            vmem((COEF, COEF), f32),
            vmem((NTYPE, COEF, COEF), f32),
            pltpu.SMEM((2,), f32),
            vmem((nx, 8, COEF), f32),
            vmem((nx, 1, COEF), f32),
            vmem((ny, 8, COEF), f32),
            vmem((ny, 8, COEF), f32),
            vmem((nx, 1, COEF), f32),
            vmem((ny, 1, COEF), f32),
            vmem((4, LX, COEF), f32),
            vmem((4, 1, COEF), f32),
            vmem((4, LX, COEF), f32),
            vmem((4, 1, COEF), f32),
            vmem((LX + 2, LY + 16, COEF), f32),
            vmem((2, 4 * ny, 8 * nx), bf16),
            vmem((2, COEF, NTYPE * COEF), bf16),
            vmem((SD, COEF), bf16),
            vmem((SD, BOXES), bf16),
            vmem((SD, COEF), f32),
            vmem((SD, COEF), i32),
            dma((10,)),
            dma((2,)),
            dma((2,)),
            dma((2,)),
            dma((2,)),
            dma((2,)),
            dma((8,)),
            dma((8,)),
            dma((SD // CHUNK,)),
        ],
        compiler_params=pltpu.CompilerParams(
            collective_id=0, has_side_effects=True, vmem_limit_bytes=48 * 1024 * 1024
        ),
        name="arnoldi_step",
    )(
        basis,
        sphere_box.reshape(SD // COEF, COEF),
        sphere_type.reshape(SD // COEF, COEF),
        near_offsets, near_mats, up_mat, top_mat, tmats, bloch_angle,
    )


def solution(mesh):
    return jax.shard_map(
        functools.partial(on_device, mesh.shape["gx"], mesh.shape["gy"]),
        mesh=mesh,
        in_specs=(
            P(None, ("gx", "gy"), None),
            P(("gx", "gy")),
            P(("gx", "gy")),
            P(),
            P(),
            P(),
            P(),
            P(),
            P(),
        ),
        out_specs=(P(("gx", "gy"), None), P()),
        check_vma=False,
    )
```

```python
import functools

import jax
import jax.numpy as jnp
from jax import lax
from jax.experimental import pallas as pl
from jax.experimental.pallas import tpu as pltpu
from jax.sharding import PartitionSpec as P

SD = 1024
LX = 16
LY = 16
KB = 3
COEF = 128
NTYPE = 8
NOFF = 9
BOXES = LX * LY
CHUNK = 256
SAMPLE = 128

MESH = pl.DeviceIdType.MESH
wave_number = 2.3
f32 = jnp.float32
bf16 = jnp.bfloat16
i32 = jnp.int32


def iota(shape, dim):
    return lax.broadcasted_iota(i32, shape, dim)


def split(x):
    high = x.astype(bf16)
    return high, (x - high.astype(f32)).astype(bf16)


def dot(a, b):
    return jnp.dot(a, b, preferred_element_type=f32)


def ones_where(mask):
    return jnp.where(mask, 1.0, 0.0).astype(bf16)


def times_i(x):
    turned = pltpu.roll(x, COEF // 2, x.ndim - 1)
    return jnp.where(iota(x.shape, x.ndim - 1) < COEF // 2, -turned, turned)


def total_lane(x, lane):
    return jnp.sum(jnp.where(iota(x.shape, 1) == lane, x, 0.0), axis=1, keepdims=True)


def to_lanes(parts):
    size = -(-len(parts) // 8) * 8
    rows = [jnp.sum(p, axis=0, keepdims=True) for p in parts]
    rows += [jnp.zeros((size - len(rows), COEF), f32)]
    sums = jnp.sum(jnp.concatenate(rows, axis=0), axis=1, keepdims=True)
    placed = jnp.where(iota((size, COEF), 0) == iota((size, COEF), 1), sums, 0.0)
    return jnp.sum(placed, axis=0, keepdims=True)


def fold(x):
    return jnp.sum(x.reshape(x.shape[0] // 8, 8, COEF), axis=0)


def far_weights(nx, ny, nz, gx, gy, theta):
    shape = (8 * ny, 8 * nz)
    m, n = iota(shape, 0), iota(shape, 1)
    grid_x, grid_y = 2 * nx, 2 * ny
    target_row = jnp.where(m >= 4 * ny, nz, 0) + gx % nz
    target_x, target_y = 2 * target_row + ((m >> 1) & 1), 2 * ((m >> 2) & (ny - 1)) + (m & 1)
    source_row = (gx // nz) * nz + (n >> 3)
    source_x, source_y = 2 * source_row + ((n >> 1) & 1), 2 * gy + (n & 1)
    shift_x = ((source_x - target_x + grid_x // 2) & (grid_x - 1)) - grid_x // 2
    shift_y = ((source_y - target_y + grid_y // 2) & (grid_y - 1)) - grid_y // 2
    wraps_x, wraps_y = target_x + shift_x - source_x, target_y + shift_y - source_y
    cross_x = jnp.where(wraps_x > 0, 1.0, jnp.where(wraps_x < 0, -1.0, 0.0))
    cross_y = jnp.where(wraps_y > 0, 1.0, jnp.where(wraps_y < 0, -1.0, 0.0))
    reach = jnp.maximum(jnp.abs(shift_x), jnp.abs(shift_y))
    distance = (shift_x * shift_x + shift_y * shift_y).astype(f32)
    radius = jnp.sqrt(jnp.maximum(distance, 1.0))
    weight = jnp.where(reach >= 2, 16.0 / radius, 0.0)
    angle = wave_number * radius + cross_x * theta[0] + cross_y * theta[1]
    return weight * jnp.where((n & 4) == 0, jnp.cos(angle), jnp.sin(angle))


def kernel(
    nx, ny,
    basis_in, box_in, type_in, offsets_in, near_in, up_in, top_in, tmats_in, bloch_in,
    out_ref, hess_ref,
    basis, box, kind, offsets, near_mats, up, top, tmats, bloch,
    ebuf, pbuf, rbuf, abuf, bbuf,
    edges, corners, rim, rim_corners, pad, far_w, top_t, hot, member_t, image, field,
    load_sem, e_sem, r_sem, a_sem, b_sem, h_send, h_recv, out_sem,
):
    gx, gy = lax.axis_index("gx"), lax.axis_index("gy")
    nz = nx // 2
    planes = 2 * ny
    half, z = gx // nz, gx % nz
    spot_in_plane = half * ny + gy
    count = float(nx * ny * SD * COEF)

    def load(src, dst, i):
        copy = pltpu.make_async_copy(src, dst, load_sem.at[i])
        copy.start()
        return copy

    load_vec = load(basis_in.at[KB - 1], basis.at[KB - 1], 0)
    load_box = load(box_in, box, 1)
    load_up = load(up_in, up, 2)
    load_bloch = load(bloch_in, bloch, 3)
    others = pl.ds(0, KB - 1)
    load_sample = load(basis_in.at[others, pl.ds(0, SAMPLE)], basis.at[others, pl.ds(0, SAMPLE)], 4)
    load_type = load(type_in, kind, 5)
    load_offsets = load(offsets_in, offsets, 6)
    load_near = load(near_in, near_mats, 7)
    load_top = load(top_in, top, 8)
    load_tmats = load(tmats_in, tmats, 9)
    rest = pl.ds(SAMPLE, SD - SAMPLE)
    load_basis = load(basis_in.at[others, rest], basis.at[others, rest], 10)

    barrier = pltpu.get_barrier_semaphore()

    def in_line(k):
        return {"gx": half * nz + (z + k) % nz}

    def in_plane(k):
        peer = (spot_in_plane + k) % planes
        return peer, {"gx": (peer // ny) * nz + z, "gy": peer % ny}

    def greet_line(k, c):
        pl.semaphore_signal(barrier, inc=1, device_id=in_line(k), device_id_type=MESH)
        return c

    def greet_plane(k, c):
        pl.semaphore_signal(barrier, inc=1, device_id=in_plane(k)[1], device_id_type=MESH)
        return c

    lax.fori_loop(1, nz, greet_line, 0)
    lax.fori_loop(1, planes, greet_plane, 0)
    sides = [(-1, 0), (1, 0), (0, -1), (0, 1), (-1, -1), (-1, 1), (1, -1), (1, 1)]

    def beside(side):
        return {"gx": (gx + side[0] + nx) % nx, "gy": (gy + side[1] + ny) % ny}

    for side in sides:
        pl.semaphore_signal(barrier, inc=1, device_id=beside(side), device_id_type=MESH)

    pending = []

    def send_line(buf, sem, rows):
        def body(k, c):
            far_half = nz // 2 + ((k + 1) // 2) * (1 - 2 * (k % 2))
            spot = buf.at[z, pl.ds(0, rows)]
            pltpu.make_async_remote_copy(
                spot, spot, sem.at[0], sem.at[1], device_id=in_line(far_half), device_id_type=MESH
            ).start()
            return c

        lax.fori_loop(0, nz - 1, body, 0)
        pending.append((buf, sem, nz - 1, rows))

    def send_plane(src, dst, sem, rows, scatter):
        def body(k, c):
            peer, device = in_plane(k)
            pltpu.make_async_remote_copy(
                src.at[peer if scatter else spot_in_plane, pl.ds(0, rows)],
                dst.at[spot_in_plane, pl.ds(0, rows)],
                sem.at[0], sem.at[1], device_id=device, device_id_type=MESH,
            ).start()
            return c

        lax.fori_loop(1, planes, body, 0)
        pending.append((src, sem, planes - 1, rows))

    def wait_all(buf, sem, number, rows):
        span = buf.at[pl.ds(0, number), pl.ds(0, rows)]
        pltpu.make_async_copy(span, span, sem).wait()

    load_box.wait()
    boxes = box[...]
    quarters = ((boxes >> 7) & 1) * 2 + ((boxes >> 3) & 1)
    quarter_of = jnp.concatenate(
        [ones_where(iota((16, COEF), 0) == quarters[r : r + 1, :]) for r in range(SD // COEF)], axis=1
    )
    load_up.wait()
    up_high, up_low = split(up[...])
    load_vec.wait()
    vector_pair = jnp.concatenate(split(basis[KB - 1]), axis=1)
    quad2 = dot(quarter_of, vector_pair)
    quad_high, quad_low = split((quad2[:, :COEF] + quad2[:, COEF:])[0:8])
    pair = jnp.concatenate([quad_high.astype(f32), quad_low.astype(f32)], axis=0).astype(bf16)
    raised = dot(pair, up_high) + dot(pair, up_low)
    ebuf[z, 0:4, :] = (raised[0:8] + raised[8:16])[0:4]
    load_sample.wait()
    sampled = [basis[k, 0:SAMPLE, :] for k in range(KB)]
    ebuf[z, 4:5, :] = to_lanes([fold(v * sampled[KB - 1]) for v in sampled])
    pl.semaphore_wait(barrier, nz + planes + 6)
    send_line(ebuf, e_sem, 5)

    member = jnp.concatenate(
        [ones_where(iota((BOXES, COEF), 0) == boxes[r : r + 1, :]) for r in range(SD // COEF)], axis=1
    )
    leaf2 = dot(member, vector_pair)
    leaf = (leaf2[:, :COEF] + leaf2[:, COEF:]).reshape(LX, LY, COEF)

    edges[0] = leaf[0]
    edges[1] = leaf[LX - 1]
    edges[2] = leaf[:, 0, :]
    edges[3] = leaf[:, LY - 1, :]
    for c, (x, y) in enumerate([(0, 0), (0, LY - 1), (LX - 1, 0), (LX - 1, LY - 1)]):
        corners[c, 0:1, :] = leaf[x, y : y + 1, :]
    halo = []
    for i, side in enumerate(sides):
        other = sides.index((-side[0], -side[1]))
        if i < 4:
            src, dst = edges.at[i], rim.at[other]
        else:
            src, dst = corners.at[i - 4], rim_corners.at[other - 4]
        copy = pltpu.make_async_remote_copy(
            src, dst, h_send.at[i], h_recv.at[other], device_id=beside(side), device_id_type=MESH
        )
        copy.start()
        halo.append(copy)
    pad[1 : LX + 1, 8 : 8 + LY, :] = leaf

    load_basis.wait()
    grams = []
    for j in range(KB):
        for k in range(j, KB):
            grams.append(fold(basis[j] * basis[k]))

    load_bloch.wait()
    theta = (bloch[0], bloch[1])
    weights = far_weights(nx, ny, nz, gx, gy, theta)
    far_w[0], far_w[1] = split(weights)

    load_type.wait()
    codes = boxes + BOXES * kind[...]
    for r in range(SD // COEF):
        code = jnp.broadcast_to(codes[r : r + 1, :], (COEF, COEF)).T
        own_box = code & (BOXES - 1)
        own_type = code >> 8
        lane = iota((COEF, COEF), 1)
        rows = pl.ds(r * COEF, COEF)
        member_t[rows, 0:COEF] = ones_where(own_box == lane)
        member_t[rows, COEF:BOXES] = ones_where(own_box == lane + COEF)
        spot = own_type * 8 + ((own_box >> 7) & 1) * 2 + ((own_box >> 3) & 1)
        hot[rows, :] = ones_where(spot == (lane & 63))
        field[rows, :] = own_type

    load_top.wait()
    load_tmats.wait()
    every = jnp.concatenate([tmats[t] for t in range(NTYPE)], axis=1)
    every_high, every_low = split(every)
    top_high, top_low = split(top[...])
    top_t[0], top_t[1] = split(dot(top_high, every_high) + dot(top_low, every_high) + dot(top_high, every_low))
    every3 = jnp.concatenate([every_high, every_high, every_low], axis=0)

    load_offsets.wait()
    load_near.wait()
    for copy in halo:
        copy.wait_recv()
    crossings = []
    row_cross = {-1: jnp.where(gx == 0, -1.0, 0.0), 0: 0.0, 1: jnp.where(gx == nx - 1, 1.0, 0.0)}
    col_cross = {-1: jnp.where(gy == 0, -1.0, 0.0), 0: 0.0, 1: jnp.where(gy == ny - 1, 1.0, 0.0)}
    angle = jnp.zeros((8, COEF), f32)
    for i, side in enumerate(sides):
        value = row_cross[side[0]] * theta[0] + col_cross[side[1]] * theta[1]
        angle = jnp.where(iota((8, COEF), 0) == i, value, angle)
    cosine, sine = jnp.cos(angle), jnp.sin(angle)

    def rotated(x, i):
        return cosine[i : i + 1] * x + sine[i : i + 1] * times_i(x)

    pad[0, 8 : 8 + LY, :] = rotated(rim[0], 0)
    pad[LX + 1, 8 : 8 + LY, :] = rotated(rim[1], 1)
    west, east = rotated(rim[2], 2), rotated(rim[3], 3)
    for x in range(LX):
        pad[x + 1, 7:8, :] = west[x : x + 1, :]
        pad[x + 1, 8 + LY : 9 + LY, :] = east[x : x + 1, :]
    for c, (x, y) in enumerate([(0, 7), (0, 8 + LY), (LX + 1, 7), (LX + 1, 8 + LY)]):
        pad[x, y : y + 1, :] = rotated(rim_corners[c], 4 + c)

    highs, lows, mats_high, mats_low = [], [], [], []
    for b in (-1, 0, 1):
        shifted = pad[:, 8 + b : 8 + b + LY, :].reshape((LX + 2) * LY, COEF)
        high, low = split(shifted)
        for a in (-1, 0, 1):
            entry = 0
            for o in range(NOFF):
                here = (offsets[0, o] == a) & (offsets[1, o] == b)
                entry = jnp.where(here, o, entry)
            mat_high, mat_low = split(near_mats[entry])
            start = (1 + a) * LY
            highs.append(high[start : start + BOXES])
            lows.append(low[start : start + BOXES])
            mats_high.append(mat_high)
            mats_low.append(mat_low)
    mat_high = jnp.concatenate(mats_high, axis=0)
    mats = jnp.concatenate([mat_high, jnp.concatenate(mats_low, axis=0)], axis=1)
    near2 = dot(jnp.concatenate(highs, axis=1), mats)
    near = near2[:, :COEF] + near2[:, COEF:] + dot(jnp.concatenate(lows, axis=1), mat_high)

    wait_all(ebuf, e_sem.at[1], nz - 1, 5)
    blocks = ebuf[...]
    sources = blocks.reshape(8 * nz, COEF)
    turned = pltpu.roll(times_i(sources), 4, 0)
    sources = jnp.where((iota(sources.shape, 0) & 4) == 0, sources, turned)
    source_high, source_low = split(sources)
    part2 = dot(far_w[0], jnp.concatenate([source_high, source_low], axis=1))
    part = part2[:, :COEF] + part2[:, COEF:] + dot(far_w[1], source_high)
    sample_sum = jnp.sum(blocks, axis=0)[4:5, :]
    for j in range(planes):
        pbuf[j, 0:4, :] = part[4 * j : 4 * j + 4]
        pbuf[j, 4:5, :] = sample_sum
    rbuf[spot_in_plane, 0:5, :] = pbuf[spot_in_plane, 0:5, :]
    send_plane(pbuf, rbuf, r_sem, 5, True)

    near_pair = jnp.concatenate(split(near), axis=1)
    for r in range(SD // CHUNK):
        rows = pl.ds(r * CHUNK, CHUNK)
        at2 = dot(member_t[rows, :], near_pair)
        at_high, at_low = split(at2[:, :COEF] + at2[:, COEF:])
        all_types = dot(jnp.concatenate([at_high, at_low, at_high], axis=1), every3)
        own_type = field[rows, :]
        value = all_types[:, :COEF]
        for t in range(1, NTYPE):
            value = jnp.where(own_type == t, all_types[:, t * COEF : (t + 1) * COEF], value)
        image[rows, :] = basis[KB - 1, rows, :] - value

    wait_all(rbuf, r_sem.at[1], planes - 1, 5)
    arrived = jnp.sum(rbuf[...], axis=0)
    far = jnp.where(iota((8, COEF), 0) < 4, arrived, 0.0)
    sample_row = arrived[4:5, :]
    far_high, far_low = split(far)
    far_pair = jnp.concatenate([far_high.astype(f32), far_low.astype(f32)], axis=0).astype(bf16)
    table2 = dot(far_pair, top_t[0]) + dot(far_pair, top_t[1])
    table = table2[0:8] + table2[8:16]
    table = jnp.concatenate([table[:, t * COEF : (t + 1) * COEF] for t in range(NTYPE)], axis=0)
    table = jnp.concatenate(split(table), axis=0)

    sample_count = float(nx * ny * SAMPLE * COEF)
    guess = [total_lane(sample_row, k) / sample_count for k in range(KB)]
    sums = [jnp.zeros((8, COEF), f32)] * (KB + 1)
    for r in range(SD // CHUNK):
        rows = pl.ds(r * CHUNK, CHUNK)
        w = image[rows, :] - dot(hot[rows, :], table)
        vectors = [basis[k, rows, :] for k in range(KB)]
        for k in range(KB):
            w = w - guess[k] * vectors[k]
        image[rows, :] = w
        for k in range(KB):
            sums[k] = sums[k] + fold(vectors[k] * w)
        sums[KB] = sums[KB] + fold(w * w)

    abuf[z, 0:1, :] = to_lanes(sums + grams)
    send_line(abuf, a_sem, 1)
    wait_all(abuf, a_sem.at[1], nz - 1, 1)
    bbuf[spot_in_plane, 0:1, :] = jnp.sum(abuf[...], axis=0)
    send_plane(bbuf, bbuf, b_sem, 1, False)
    wait_all(bbuf, b_sem.at[1], planes - 1, 1)
    totals = jnp.sum(bbuf[...], axis=0)
    inner = [total_lane(totals, k) for k in range(KB)]
    square = total_lane(totals, KB)
    gram, lane = {}, KB + 1
    for j in range(KB):
        for k in range(j, KB):
            gram[j, k] = gram[k, j] = total_lane(totals, lane)
            lane += 1
    coeffs = []
    for k in range(KB):
        value = inner[k]
        for j in range(KB):
            value = value + gram[k, j] * guess[j]
        coeffs.append(value / count)
    step = [coeffs[k] - guess[k] for k in range(KB)]
    for k in range(KB):
        along = -2.0 * inner[k]
        for j in range(KB):
            along = along + gram[k, j] * step[j]
        square = square + step[k] * along
    beta = jnp.sqrt(jnp.maximum(square, 0.0) / count + 1e-06)
    scale = 1.0 / beta

    outs = []
    for r in range(SD // CHUNK):
        rows = pl.ds(r * CHUNK, CHUNK)
        w = image[rows, :]
        for k in range(KB):
            w = w - step[k] * basis[k, rows, :]
        image[rows, :] = w * scale
        copy = pltpu.make_async_copy(image.at[rows], out_ref.at[rows], out_sem.at[r])
        copy.start()
        outs.append(copy)
    for k, value in enumerate(coeffs + [beta]):
        hess_ref[k] = jnp.sum(value)
    for copy in halo:
        copy.wait_send()
    for buf, sem, number, rows in pending:
        wait_all(buf, sem.at[0], number, rows)
    for copy in outs:
        copy.wait()


def on_device(nx, ny, basis, sphere_box, sphere_type, near_offsets, near_mats, up_mat, top_mat, tmats, bloch_angle):
    nz = nx // 2
    vmem, dma = pltpu.VMEM, pltpu.SemaphoreType.DMA
    return pl.pallas_call(
        functools.partial(kernel, nx, ny),
        out_shape=(jax.ShapeDtypeStruct((SD, COEF), f32), jax.ShapeDtypeStruct((KB + 1,), f32)),
        in_specs=[pl.BlockSpec(memory_space=pltpu.HBM)] * 9,
        out_specs=(pl.BlockSpec(memory_space=pltpu.HBM), pl.BlockSpec(memory_space=pltpu.SMEM)),
        scratch_shapes=[
            vmem((KB, SD, COEF), f32),
            vmem((SD // COEF, COEF), i32),
            vmem((SD // COEF, COEF), i32),
            pltpu.SMEM((2, NOFF), i32),
            vmem((NOFF, COEF, COEF), f32),
            vmem((COEF, COEF), f32),
            vmem((COEF, COEF), f32),
            vmem((NTYPE, COEF, COEF), f32),
            pltpu.SMEM((2,), f32),
            vmem((nz, 8, COEF), f32),
            vmem((2 * ny, 8, COEF), f32),
            vmem((2 * ny, 8, COEF), f32),
            vmem((nz, 1, COEF), f32),
            vmem((2 * ny, 1, COEF), f32),
            vmem((4, LX, COEF), f32),
            vmem((4, 1, COEF), f32),
            vmem((4, LX, COEF), f32),
            vmem((4, 1, COEF), f32),
            vmem((LX + 2, LY + 16, COEF), f32),
            vmem((2, 8 * ny, 8 * nz), bf16),
            vmem((2, COEF, NTYPE * COEF), bf16),
            vmem((SD, COEF), bf16),
            vmem((SD, BOXES), bf16),
            vmem((SD, COEF), f32),
            vmem((SD, COEF), i32),
            dma((11,)),
            dma((2,)),
            dma((2,)),
            dma((2,)),
            dma((2,)),
            dma((8,)),
            dma((8,)),
            dma((SD // CHUNK,)),
        ],
        compiler_params=pltpu.CompilerParams(
            collective_id=0, has_side_effects=True, vmem_limit_bytes=64 * 1024 * 1024
        ),
        name="arnoldi_step",
    )(
        basis,
        sphere_box.reshape(SD // COEF, COEF),
        sphere_type.reshape(SD // COEF, COEF),
        near_offsets.T, near_mats, up_mat, top_mat, tmats, bloch_angle,
    )


def solution(mesh):
    return jax.shard_map(
        functools.partial(on_device, mesh.shape["gx"], mesh.shape["gy"]),
        mesh=mesh,
        in_specs=(
            P(None, ("gx", "gy"), None),
            P(("gx", "gy")),
            P(("gx", "gy")),
            P(),
            P(),
            P(),
            P(),
            P(),
            P(),
        ),
        out_specs=(P(("gx", "gy"), None), P()),
        check_vma=False,
    )
```

```python
import functools

import jax
import jax.numpy as jnp
from jax import lax
from jax.experimental import pallas as pl
from jax.experimental.pallas import tpu as pltpu
from jax.sharding import PartitionSpec as P

SD = 1024
LX = 16
LY = 16
KB = 3
COEF = 128
NTYPE = 8
NOFF = 9
BOXES = LX * LY
CHUNK = 256
SAMPLE = 128

MESH = pl.DeviceIdType.MESH
wave_number = 2.3
f32 = jnp.float32
bf16 = jnp.bfloat16
i32 = jnp.int32


def iota(shape, dim):
    return lax.broadcasted_iota(i32, shape, dim)


def split(x):
    high = x.astype(bf16)
    return high, (x - high.astype(f32)).astype(bf16)


def dot(a, b):
    return jnp.dot(a, b, preferred_element_type=f32)


def ones_where(mask):
    return jnp.where(mask, 1.0, 0.0).astype(bf16)


def times_i(x):
    turned = pltpu.roll(x, COEF // 2, x.ndim - 1)
    return jnp.where(iota(x.shape, x.ndim - 1) < COEF // 2, -turned, turned)


def total_lane(x, lane):
    return jnp.sum(jnp.where(iota(x.shape, 1) == lane, x, 0.0), axis=1, keepdims=True)


def to_lanes(parts):
    size = -(-len(parts) // 8) * 8
    rows = [jnp.sum(p, axis=0, keepdims=True) for p in parts]
    rows += [jnp.zeros((size - len(rows), COEF), f32)]
    sums = jnp.sum(jnp.concatenate(rows, axis=0), axis=1, keepdims=True)
    placed = jnp.where(iota((size, COEF), 0) == iota((size, COEF), 1), sums, 0.0)
    return jnp.sum(placed, axis=0, keepdims=True)


def fold(x):
    return jnp.sum(x.reshape(x.shape[0] // 8, 8, COEF), axis=0)


def far_weights(nx, ny, nz, gx, gy, theta):
    shape = (8 * ny, 8 * nz)
    m, n = iota(shape, 0), iota(shape, 1)
    grid_x, grid_y = 2 * nx, 2 * ny
    target_row = jnp.where(m >= 4 * ny, nz, 0) + gx % nz
    target_x, target_y = 2 * target_row + ((m >> 1) & 1), 2 * ((m >> 2) & (ny - 1)) + (m & 1)
    source_row = (gx // nz) * nz + (n >> 3)
    source_x, source_y = 2 * source_row + ((n >> 1) & 1), 2 * gy + (n & 1)
    shift_x = ((source_x - target_x + grid_x // 2) & (grid_x - 1)) - grid_x // 2
    shift_y = ((source_y - target_y + grid_y // 2) & (grid_y - 1)) - grid_y // 2
    wraps_x, wraps_y = target_x + shift_x - source_x, target_y + shift_y - source_y
    cross_x = jnp.where(wraps_x > 0, 1.0, jnp.where(wraps_x < 0, -1.0, 0.0))
    cross_y = jnp.where(wraps_y > 0, 1.0, jnp.where(wraps_y < 0, -1.0, 0.0))
    reach = jnp.maximum(jnp.abs(shift_x), jnp.abs(shift_y))
    distance = (shift_x * shift_x + shift_y * shift_y).astype(f32)
    radius = jnp.sqrt(jnp.maximum(distance, 1.0))
    weight = jnp.where(reach >= 2, 16.0 / radius, 0.0)
    angle = wave_number * radius + cross_x * theta[0] + cross_y * theta[1]
    return weight * jnp.where((n & 4) == 0, jnp.cos(angle), jnp.sin(angle))


def kernel(
    nx, ny,
    basis_in, box_in, type_in, offsets_in, near_in, up_in, top_in, tmats_in, bloch_in,
    out_ref, hess_ref,
    basis, box, kind, offsets, near_mats, up, top, tmats, bloch,
    ebuf, pbuf, rbuf, abuf, bbuf,
    edges, corners, rim, rim_corners, pad, far_w, top_t, hot, member_t, image, field,
    load_sem, e_sem, r_sem, a_sem, b_sem, h_send, h_recv, out_sem,
):
    gx, gy = lax.axis_index("gx"), lax.axis_index("gy")
    nz = nx // 2
    planes = 2 * ny
    half, z = gx // nz, gx % nz
    spot_in_plane = half * ny + gy
    count = float(nx * ny * SD * COEF)

    def load(src, dst, i):
        copy = pltpu.make_async_copy(src, dst, load_sem.at[i])
        copy.start()
        return copy

    load_vec = load(basis_in.at[KB - 1], basis.at[KB - 1], 0)
    load_box = load(box_in, box, 1)
    load_up = load(up_in, up, 2)
    load_bloch = load(bloch_in, bloch, 3)
    others = pl.ds(0, KB - 1)
    load_sample = load(basis_in.at[others, pl.ds(0, SAMPLE)], basis.at[others, pl.ds(0, SAMPLE)], 4)
    load_type = load(type_in, kind, 5)
    load_offsets = load(offsets_in, offsets, 6)
    load_near = load(near_in, near_mats, 7)
    load_top = load(top_in, top, 8)
    load_tmats = load(tmats_in, tmats, 9)
    rest = pl.ds(SAMPLE, SD - SAMPLE)
    load_basis = load(basis_in.at[others, rest], basis.at[others, rest], 10)

    barrier = pltpu.get_barrier_semaphore()

    def in_line(k):
        return {"gx": half * nz + (z + k) % nz}

    def in_plane(k):
        peer = (spot_in_plane + k) % planes
        return peer, {"gx": (peer // ny) * nz + z, "gy": peer % ny}

    def greet_line(k, c):
        pl.semaphore_signal(barrier, inc=1, device_id=in_line(k), device_id_type=MESH)
        return c

    def greet_plane(k, c):
        pl.semaphore_signal(barrier, inc=1, device_id=in_plane(k)[1], device_id_type=MESH)
        return c

    lax.fori_loop(1, nz, greet_line, 0)
    lax.fori_loop(1, planes, greet_plane, 0)
    sides = [(-1, 0), (1, 0), (0, -1), (0, 1), (-1, -1), (-1, 1), (1, -1), (1, 1)]

    def beside(side):
        return {"gx": (gx + side[0] + nx) % nx, "gy": (gy + side[1] + ny) % ny}

    for side in sides:
        pl.semaphore_signal(barrier, inc=1, device_id=beside(side), device_id_type=MESH)

    pending = []

    def send_line(buf, sem, rows):
        def body(k, c):
            far_half = nz // 2 + ((k + 1) // 2) * (1 - 2 * (k % 2))
            spot = buf.at[z, pl.ds(0, rows)]
            pltpu.make_async_remote_copy(
                spot, spot, sem.at[0], sem.at[1], device_id=in_line(far_half), device_id_type=MESH
            ).start()
            return c

        lax.fori_loop(0, nz - 1, body, 0)
        pending.append((buf, sem, nz - 1, rows))

    def send_plane(src, dst, sem, rows, scatter):
        def body(k, c):
            peer, device = in_plane(k)
            pltpu.make_async_remote_copy(
                src.at[peer if scatter else spot_in_plane, pl.ds(0, rows)],
                dst.at[spot_in_plane, pl.ds(0, rows)],
                sem.at[0], sem.at[1], device_id=device, device_id_type=MESH,
            ).start()
            return c

        lax.fori_loop(1, planes, body, 0)
        pending.append((src, sem, planes - 1, rows))

    def wait_all(buf, sem, number, rows):
        span = buf.at[pl.ds(0, number), pl.ds(0, rows)]
        pltpu.make_async_copy(span, span, sem).wait()

    load_box.wait()
    boxes = box[...]
    quarters = ((boxes >> 7) & 1) * 2 + ((boxes >> 3) & 1)
    quarter_of = jnp.concatenate(
        [ones_where(iota((16, COEF), 0) == quarters[r : r + 1, :]) for r in range(SD // COEF)], axis=1
    )
    load_up.wait()
    up_high, up_low = split(up[...])
    load_vec.wait()
    vector_pair = jnp.concatenate(split(basis[KB - 1]), axis=1)
    quad2 = dot(quarter_of, vector_pair)
    quad_high, quad_low = split((quad2[:, :COEF] + quad2[:, COEF:])[0:8])
    pair = jnp.concatenate([quad_high.astype(f32), quad_low.astype(f32)], axis=0).astype(bf16)
    raised = dot(pair, up_high) + dot(pair, up_low)
    ebuf[z, 0:4, :] = (raised[0:8] + raised[8:16])[0:4]
    load_sample.wait()
    sampled = [basis[k, 0:SAMPLE, :] for k in range(KB)]
    ebuf[z, 4:5, :] = to_lanes([fold(v * sampled[KB - 1]) for v in sampled])
    pl.semaphore_wait(barrier, nz + planes + 6)
    send_line(ebuf, e_sem, 5)

    member = jnp.concatenate(
        [ones_where(iota((BOXES, COEF), 0) == boxes[r : r + 1, :]) for r in range(SD // COEF)], axis=1
    )
    leaf2 = dot(member, vector_pair)
    leaf = (leaf2[:, :COEF] + leaf2[:, COEF:]).reshape(LX, LY, COEF)

    edges[0] = leaf[0]
    edges[1] = leaf[LX - 1]
    edges[2] = leaf[:, 0, :]
    edges[3] = leaf[:, LY - 1, :]
    for c, (x, y) in enumerate([(0, 0), (0, LY - 1), (LX - 1, 0), (LX - 1, LY - 1)]):
        corners[c, 0:1, :] = leaf[x, y : y + 1, :]
    halo = []
    for i, side in enumerate(sides):
        other = sides.index((-side[0], -side[1]))
        if i < 4:
            src, dst = edges.at[i], rim.at[other]
        else:
            src, dst = corners.at[i - 4], rim_corners.at[other - 4]
        copy = pltpu.make_async_remote_copy(
            src, dst, h_send.at[i], h_recv.at[other], device_id=beside(side), device_id_type=MESH
        )
        copy.start()
        halo.append(copy)
    pad[1 : LX + 1, 8 : 8 + LY, :] = leaf

    load_basis.wait()
    grams = []
    for j in range(KB):
        for k in range(j, KB):
            grams.append(fold(basis[j] * basis[k]))

    load_bloch.wait()
    theta = (bloch[0], bloch[1])
    weights = far_weights(nx, ny, nz, gx, gy, theta)
    far_w[0], far_w[1] = split(weights)

    load_type.wait()
    codes = boxes + BOXES * kind[...]
    for r in range(SD // COEF):
        code = jnp.broadcast_to(codes[r : r + 1, :], (COEF, COEF)).T
        own_box = code & (BOXES - 1)
        own_type = code >> 8
        lane = iota((COEF, COEF), 1)
        rows = pl.ds(r * COEF, COEF)
        member_t[rows, 0:COEF] = ones_where(own_box == lane)
        member_t[rows, COEF:BOXES] = ones_where(own_box == lane + COEF)
        spot = own_type * 8 + ((own_box >> 7) & 1) * 2 + ((own_box >> 3) & 1)
        hot[rows, :] = ones_where(spot == (lane & 63))
        field[rows, :] = own_type

    load_top.wait()
    load_tmats.wait()
    every = jnp.concatenate([tmats[t] for t in range(NTYPE)], axis=1)
    every_high, every_low = split(every)
    top_high, top_low = split(top[...])
    top_t[0], top_t[1] = split(dot(top_high, every_high) + dot(top_low, every_high) + dot(top_high, every_low))
    every3 = jnp.concatenate([every_high, every_high, every_low], axis=0)

    load_offsets.wait()
    load_near.wait()
    for copy in halo:
        copy.wait_recv()
    crossings = []
    row_cross = {-1: jnp.where(gx == 0, -1.0, 0.0), 0: 0.0, 1: jnp.where(gx == nx - 1, 1.0, 0.0)}
    col_cross = {-1: jnp.where(gy == 0, -1.0, 0.0), 0: 0.0, 1: jnp.where(gy == ny - 1, 1.0, 0.0)}
    angle = jnp.zeros((8, COEF), f32)
    for i, side in enumerate(sides):
        value = row_cross[side[0]] * theta[0] + col_cross[side[1]] * theta[1]
        angle = jnp.where(iota((8, COEF), 0) == i, value, angle)
    cosine, sine = jnp.cos(angle), jnp.sin(angle)

    def rotated(x, i):
        return cosine[i : i + 1] * x + sine[i : i + 1] * times_i(x)

    pad[0, 8 : 8 + LY, :] = rotated(rim[0], 0)
    pad[LX + 1, 8 : 8 + LY, :] = rotated(rim[1], 1)
    west, east = rotated(rim[2], 2), rotated(rim[3], 3)
    for x in range(LX):
        pad[x + 1, 7:8, :] = west[x : x + 1, :]
        pad[x + 1, 8 + LY : 9 + LY, :] = east[x : x + 1, :]
    for c, (x, y) in enumerate([(0, 7), (0, 8 + LY), (LX + 1, 7), (LX + 1, 8 + LY)]):
        pad[x, y : y + 1, :] = rotated(rim_corners[c], 4 + c)

    highs, lows, mats_high, mats_low = [], [], [], []
    for b in (-1, 0, 1):
        shifted = pad[:, 8 + b : 8 + b + LY, :].reshape((LX + 2) * LY, COEF)
        high, low = split(shifted)
        for a in (-1, 0, 1):
            entry = 0
            for o in range(NOFF):
                here = (offsets[0, o] == a) & (offsets[1, o] == b)
                entry = jnp.where(here, o, entry)
            mat_high, mat_low = split(near_mats[entry])
            start = (1 + a) * LY
            highs.append(high[start : start + BOXES])
            lows.append(low[start : start + BOXES])
            mats_high.append(mat_high)
            mats_low.append(mat_low)
    mat_high = jnp.concatenate(mats_high, axis=0)
    mats = jnp.concatenate([mat_high, jnp.concatenate(mats_low, axis=0)], axis=1)
    near2 = dot(jnp.concatenate(highs, axis=1), mats)
    near = near2[:, :COEF] + near2[:, COEF:] + dot(jnp.concatenate(lows, axis=1), mat_high)

    wait_all(ebuf, e_sem.at[1], nz - 1, 5)
    blocks = ebuf[...]
    sources = blocks.reshape(8 * nz, COEF)
    turned = pltpu.roll(times_i(sources), 4, 0)
    sources = jnp.where((iota(sources.shape, 0) & 4) == 0, sources, turned)
    source_high, source_low = split(sources)
    part2 = dot(far_w[0], jnp.concatenate([source_high, source_low], axis=1))
    part = part2[:, :COEF] + part2[:, COEF:] + dot(far_w[1], source_high)
    sample_sum = jnp.sum(blocks, axis=0)[4:5, :]
    for j in range(planes):
        pbuf[j, 0:4, :] = part[4 * j : 4 * j + 4]
        pbuf[j, 4:5, :] = sample_sum
    rbuf[spot_in_plane, 0:5, :] = pbuf[spot_in_plane, 0:5, :]
    send_plane(pbuf, rbuf, r_sem, 5, True)

    near_pair = jnp.concatenate(split(near), axis=1)
    for r in range(SD // CHUNK):
        rows = pl.ds(r * CHUNK, CHUNK)
        at2 = dot(member_t[rows, :], near_pair)
        at_high, at_low = split(at2[:, :COEF] + at2[:, COEF:])
        all_types = dot(jnp.concatenate([at_high, at_low, at_high], axis=1), every3)
        own_type = field[rows, :]
        value = all_types[:, :COEF]
        for t in range(1, NTYPE):
            value = jnp.where(own_type == t, all_types[:, t * COEF : (t + 1) * COEF], value)
        image[rows, :] = basis[KB - 1, rows, :] - value

    wait_all(rbuf, r_sem.at[1], planes - 1, 5)
    arrived = jnp.sum(rbuf[...], axis=0)
    far = jnp.where(iota((8, COEF), 0) < 4, arrived, 0.0)
    sample_row = arrived[4:5, :]
    far_high, far_low = split(far)
    far_pair = jnp.concatenate([far_high.astype(f32), far_low.astype(f32)], axis=0).astype(bf16)
    table2 = dot(far_pair, top_t[0]) + dot(far_pair, top_t[1])
    table = table2[0:8] + table2[8:16]
    table = jnp.concatenate([table[:, t * COEF : (t + 1) * COEF] for t in range(NTYPE)], axis=0)
    table = jnp.concatenate(split(table), axis=0)

    sample_count = float(nx * ny * SAMPLE * COEF)
    guess = [total_lane(sample_row, k) / sample_count for k in range(KB)]
    sums = [jnp.zeros((8, COEF), f32)] * (KB + 1)
    for r in range(SD // CHUNK):
        rows = pl.ds(r * CHUNK, CHUNK)
        w = image[rows, :] - dot(hot[rows, :], table)
        vectors = [basis[k, rows, :] for k in range(KB)]
        for k in range(KB):
            w = w - guess[k] * vectors[k]
        image[rows, :] = w
        for k in range(KB):
            sums[k] = sums[k] + fold(vectors[k] * w)
        sums[KB] = sums[KB] + fold(w * w)

    abuf[z, 0:1, :] = to_lanes(sums + grams)
    send_line(abuf, a_sem, 1)
    wait_all(abuf, a_sem.at[1], nz - 1, 1)
    bbuf[spot_in_plane, 0:1, :] = jnp.sum(abuf[...], axis=0)
    send_plane(bbuf, bbuf, b_sem, 1, False)
    wait_all(bbuf, b_sem.at[1], planes - 1, 1)
    totals = jnp.sum(bbuf[...], axis=0)
    inner = [total_lane(totals, k) for k in range(KB)]
    square = total_lane(totals, KB)
    gram, lane = {}, KB + 1
    for j in range(KB):
        for k in range(j, KB):
            gram[j, k] = gram[k, j] = total_lane(totals, lane)
            lane += 1
    coeffs = []
    for k in range(KB):
        value = inner[k]
        for j in range(KB):
            value = value + gram[k, j] * guess[j]
        coeffs.append(value / count)
    step = [coeffs[k] - guess[k] for k in range(KB)]
    for k in range(KB):
        along = -2.0 * inner[k]
        for j in range(KB):
            along = along + gram[k, j] * step[j]
        square = square + step[k] * along
    beta = jnp.sqrt(jnp.maximum(square, 0.0) / count + 1e-06)
    scale = 1.0 / beta

    outs = []
    for r in range(SD // CHUNK):
        rows = pl.ds(r * CHUNK, CHUNK)
        w = image[rows, :]
        for k in range(KB):
            w = w - step[k] * basis[k, rows, :]
        out_ref[rows, :] = w * scale
    for k, value in enumerate(coeffs + [beta]):
        hess_ref[k] = jnp.sum(value)
    for copy in halo:
        copy.wait_send()
    for buf, sem, number, rows in pending:
        wait_all(buf, sem.at[0], number, rows)
    for copy in outs:
        copy.wait()


def on_device(nx, ny, basis, sphere_box, sphere_type, near_offsets, near_mats, up_mat, top_mat, tmats, bloch_angle):
    nz = nx // 2
    vmem, dma = pltpu.VMEM, pltpu.SemaphoreType.DMA
    return pl.pallas_call(
        functools.partial(kernel, nx, ny),
        out_shape=(pltpu.VMEM((SD, COEF), f32), pltpu.SMEM((KB + 1,), f32)),
        in_specs=[pl.BlockSpec(memory_space=pltpu.HBM)] * 9,
        out_specs=(pl.BlockSpec(memory_space=pltpu.VMEM), pl.BlockSpec(memory_space=pltpu.SMEM)),
        scratch_shapes=[
            vmem((KB, SD, COEF), f32),
            vmem((SD // COEF, COEF), i32),
            vmem((SD // COEF, COEF), i32),
            pltpu.SMEM((2, NOFF), i32),
            vmem((NOFF, COEF, COEF), f32),
            vmem((COEF, COEF), f32),
            vmem((COEF, COEF), f32),
            vmem((NTYPE, COEF, COEF), f32),
            pltpu.SMEM((2,), f32),
            vmem((nz, 8, COEF), f32),
            vmem((2 * ny, 8, COEF), f32),
            vmem((2 * ny, 8, COEF), f32),
            vmem((nz, 1, COEF), f32),
            vmem((2 * ny, 1, COEF), f32),
            vmem((4, LX, COEF), f32),
            vmem((4, 1, COEF), f32),
            vmem((4, LX, COEF), f32),
            vmem((4, 1, COEF), f32),
            vmem((LX + 2, LY + 16, COEF), f32),
            vmem((2, 8 * ny, 8 * nz), bf16),
            vmem((2, COEF, NTYPE * COEF), bf16),
            vmem((SD, COEF), bf16),
            vmem((SD, BOXES), bf16),
            vmem((SD, COEF), f32),
            vmem((SD, COEF), i32),
            dma((11,)),
            dma((2,)),
            dma((2,)),
            dma((2,)),
            dma((2,)),
            dma((8,)),
            dma((8,)),
            dma((SD // CHUNK,)),
        ],
        compiler_params=pltpu.CompilerParams(
            collective_id=0, has_side_effects=True, vmem_limit_bytes=48 * 1024 * 1024
        ),
        name="arnoldi_step",
    )(
        *[pltpu.with_memory_space_constraint(x, pltpu.HBM) for x in (basis,
        sphere_box.reshape(SD // COEF, COEF),
        sphere_type.reshape(SD // COEF, COEF),
        near_offsets.T, near_mats, up_mat, top_mat, tmats, bloch_angle)]
    )


def solution(mesh):
    return jax.shard_map(
        functools.partial(on_device, mesh.shape["gx"], mesh.shape["gy"]),
        mesh=mesh,
        in_specs=(
            P(None, ("gx", "gy"), None),
            P(("gx", "gy")),
            P(("gx", "gy")),
            P(),
            P(),
            P(),
            P(),
            P(),
            P(),
        ),
        out_specs=(P(("gx", "gy"), None), P()),
        check_vma=False,
    )
```

```python
import functools

import jax
import jax.numpy as jnp
from jax import lax
from jax.experimental import pallas as pl
from jax.experimental.pallas import tpu as pltpu
from jax.sharding import PartitionSpec as P

SD = 1024
LX = 16
LY = 16
KB = 3
COEF = 128
NTYPE = 8
NOFF = 9
BOXES = LX * LY
CHUNK = 256
SAMPLE = 128

MESH = pl.DeviceIdType.MESH
wave_number = 2.3
f32 = jnp.float32
bf16 = jnp.bfloat16
i32 = jnp.int32


def iota(shape, dim):
    return lax.broadcasted_iota(i32, shape, dim)


def split(x):
    high = x.astype(bf16)
    return high, (x - high.astype(f32)).astype(bf16)


def dot(a, b):
    return jnp.dot(a, b, preferred_element_type=f32)


def ones_where(mask):
    return jnp.where(mask, 1.0, 0.0).astype(bf16)


def times_i(x):
    turned = pltpu.roll(x, COEF // 2, x.ndim - 1)
    return jnp.where(iota(x.shape, x.ndim - 1) < COEF // 2, -turned, turned)


def total_lane(x, lane):
    return jnp.sum(jnp.where(iota(x.shape, 1) == lane, x, 0.0), axis=1, keepdims=True)


def to_lanes(parts):
    size = -(-len(parts) // 8) * 8
    rows = [jnp.sum(p, axis=0, keepdims=True) for p in parts]
    rows += [jnp.zeros((size - len(rows), COEF), f32)]
    sums = jnp.sum(jnp.concatenate(rows, axis=0), axis=1, keepdims=True)
    placed = jnp.where(iota((size, COEF), 0) == iota((size, COEF), 1), sums, 0.0)
    return jnp.sum(placed, axis=0, keepdims=True)


def fold(x):
    return jnp.sum(x.reshape(x.shape[0] // 8, 8, COEF), axis=0)


def far_weights(nx, ny, nz, gx, gy, theta):
    shape = (4 * nz, 16 * ny)
    m, n = iota(shape, 0), iota(shape, 1)
    grid_x, grid_y = 2 * nx, 2 * ny
    target_row = (gx // nz) * nz + (m >> 2)
    target_x, target_y = 2 * target_row + ((m >> 1) & 1), 2 * gy + (m & 1)
    source_row = jnp.where(n >= 8 * ny, nz, 0) + gx % nz
    source_x, source_y = 2 * source_row + ((n >> 1) & 1), 2 * ((n >> 3) & (ny - 1)) + (n & 1)
    shift_x = ((source_x - target_x + grid_x // 2) & (grid_x - 1)) - grid_x // 2
    shift_y = ((source_y - target_y + grid_y // 2) & (grid_y - 1)) - grid_y // 2
    wraps_x, wraps_y = target_x + shift_x - source_x, target_y + shift_y - source_y
    cross_x = jnp.where(wraps_x > 0, 1.0, jnp.where(wraps_x < 0, -1.0, 0.0))
    cross_y = jnp.where(wraps_y > 0, 1.0, jnp.where(wraps_y < 0, -1.0, 0.0))
    reach = jnp.maximum(jnp.abs(shift_x), jnp.abs(shift_y))
    distance = (shift_x * shift_x + shift_y * shift_y).astype(f32)
    radius = jnp.sqrt(jnp.maximum(distance, 1.0))
    weight = jnp.where(reach >= 2, 16.0 / radius, 0.0)
    angle = wave_number * radius + cross_x * theta[0] + cross_y * theta[1]
    return weight * jnp.where((n & 4) == 0, jnp.cos(angle), jnp.sin(angle))


def kernel(
    nx, ny,
    basis_in, box_in, type_in, offsets_in, near_in, up_in, top_in, tmats_in, bloch_in,
    out_ref, hess_ref,
    basis, box, kind, offsets, near_mats, up, top, tmats, bloch,
    ebuf, pbuf, rbuf, abuf, bbuf,
    edges, corners, rim, rim_corners, pad, far_w, top_t, hot, member_t, image, field,
    load_sem, e_sem, r_sem, a_sem, b_sem, h_send, h_recv, met,
):
    gx, gy = lax.axis_index("gx"), lax.axis_index("gy")
    nz = nx // 2
    planes = 2 * ny
    half, z = gx // nz, gx % nz
    spot_in_plane = half * ny + gy
    count = float(nx * ny * SD * COEF)

    def load(src, dst, i):
        copy = pltpu.make_async_copy(src, dst, load_sem.at[i])
        copy.start()
        return copy

    load_vec = load(basis_in.at[KB - 1], basis.at[KB - 1], 0)
    load_box = load(box_in, box, 1)
    load_up = load(up_in, up, 2)
    load_bloch = load(bloch_in, bloch, 3)
    others = pl.ds(0, KB - 1)
    load_sample = load(basis_in.at[others, pl.ds(0, SAMPLE)], basis.at[others, pl.ds(0, SAMPLE)], 4)
    load_type = load(type_in, kind, 5)
    load_offsets = load(offsets_in, offsets, 6)
    load_near = load(near_in, near_mats, 7)
    load_top = load(top_in, top, 8)
    load_tmats = load(tmats_in, tmats, 9)
    rest = pl.ds(SAMPLE, SD - SAMPLE)
    load_basis = load(basis_in.at[others, rest], basis.at[others, rest], 10)

    barrier = pltpu.get_barrier_semaphore()

    def in_line(k):
        return {"gx": half * nz + (z + k) % nz}

    def in_plane(k):
        peer = (spot_in_plane + k) % planes
        return peer, {"gx": (peer // ny) * nz + z, "gy": peer % ny}

    def greet_plane(k, c):
        pl.semaphore_signal(barrier, inc=1, device_id=in_plane(k)[1], device_id_type=MESH)
        return c

    reach = nz // 4
    for k in range(1, reach + 1):
        for way in (k, nz - k):
            pl.semaphore_signal(barrier, inc=1, device_id=in_line(way), device_id_type=MESH)
    lax.fori_loop(1, planes, greet_plane, 0)
    sides = [(-1, 0), (1, 0), (0, -1), (0, 1), (-1, -1), (-1, 1), (1, -1), (1, 1)]

    def beside(side):
        return {"gx": (gx + side[0] + nx) % nx, "gy": (gy + side[1] + ny) % ny}

    for side in sides[:2] + sides[4:]:
        pl.semaphore_signal(barrier, inc=1, device_id=beside(side), device_id_type=MESH)

    pending = []

    def send_line(src, dst, sem, rows, scatter):
        def body(k, c):
            far_half = nz // 2 + ((k + 1) // 2) * (1 - 2 * (k % 2))
            peer = (z + far_half) % nz
            pltpu.make_async_remote_copy(
                src.at[peer if scatter else z, pl.ds(0, rows)],
                dst.at[z, pl.ds(0, rows)],
                sem.at[0], sem.at[1], device_id=in_line(far_half), device_id_type=MESH,
            ).start()
            return c

        lax.fori_loop(0, nz - 1, body, 0)
        pending.append((src, sem, nz - 1, rows))

    def send_plane(src, dst, sem, rows, scatter):
        def body(k, c):
            peer, device = in_plane(k)
            pltpu.make_async_remote_copy(
                src.at[peer if scatter else spot_in_plane, pl.ds(0, rows)],
                dst.at[spot_in_plane, pl.ds(0, rows)],
                sem.at[0], sem.at[1], device_id=device, device_id_type=MESH,
            ).start()
            return c

        lax.fori_loop(1, planes, body, 0)
        pending.append((src, sem, planes - 1, rows))

    def wait_all(buf, sem, number, rows):
        span = buf.at[pl.ds(0, number), pl.ds(0, rows)]
        pltpu.make_async_copy(span, span, sem).wait()

    load_box.wait()
    boxes = box[...]
    quarters = ((boxes >> 7) & 1) * 2 + ((boxes >> 3) & 1)
    quarter_of = jnp.concatenate(
        [ones_where(iota((16, COEF), 0) == quarters[r : r + 1, :]) for r in range(SD // COEF)], axis=1
    )
    load_up.wait()
    up_high, up_low = split(up[...])
    load_vec.wait()
    vector_pair = jnp.concatenate(split(basis[KB - 1]), axis=1)
    quad2 = dot(quarter_of, vector_pair)
    quad_high, quad_low = split((quad2[:, :COEF] + quad2[:, COEF:])[0:8])
    pair = jnp.concatenate([quad_high.astype(f32), quad_low.astype(f32)], axis=0).astype(bf16)
    raised = dot(pair, up_high) + dot(pair, up_low)
    ebuf[spot_in_plane, 0:4, :] = (raised[0:8] + raised[8:16])[0:4]
    load_sample.wait()
    sampled = [basis[k, 0:SAMPLE, :] for k in range(KB)]
    ebuf[spot_in_plane, 4:5, :] = to_lanes([fold(v * sampled[KB - 1]) for v in sampled])
    pl.semaphore_wait(barrier, 2 * reach + planes - 1 + 6)
    send_plane(ebuf, ebuf, e_sem, 5, False)
    for i, way in enumerate((reach, nz - reach)):
        pl.semaphore_signal(met.at[i], inc=1, device_id=in_line(way), device_id_type=MESH)

    member = jnp.concatenate(
        [ones_where(iota((BOXES, COEF), 0) == boxes[r : r + 1, :]) for r in range(SD // COEF)], axis=1
    )
    leaf2 = dot(member, vector_pair)
    leaf = (leaf2[:, :COEF] + leaf2[:, COEF:]).reshape(LX, LY, COEF)

    edges[0] = leaf[0]
    edges[1] = leaf[LX - 1]
    edges[2] = leaf[:, 0, :]
    edges[3] = leaf[:, LY - 1, :]
    for c, (x, y) in enumerate([(0, 0), (0, LY - 1), (LX - 1, 0), (LX - 1, LY - 1)]):
        corners[c, 0:1, :] = leaf[x, y : y + 1, :]
    halo = []
    for i, side in enumerate(sides):
        other = sides.index((-side[0], -side[1]))
        if i < 4:
            src, dst = edges.at[i], rim.at[other]
        else:
            src, dst = corners.at[i - 4], rim_corners.at[other - 4]
        copy = pltpu.make_async_remote_copy(
            src, dst, h_send.at[i], h_recv.at[other], device_id=beside(side), device_id_type=MESH
        )
        copy.start()
        halo.append(copy)
    pad[1 : LX + 1, 8 : 8 + LY, :] = leaf

    load_basis.wait()
    grams = []
    for j in range(KB):
        for k in range(j, KB):
            grams.append(fold(basis[j] * basis[k]))

    load_bloch.wait()
    theta = (bloch[0], bloch[1])
    weights = far_weights(nx, ny, nz, gx, gy, theta)
    far_w[0], far_w[1] = split(weights)

    load_type.wait()
    codes = boxes + BOXES * kind[...]
    for r in range(SD // COEF):
        code = jnp.broadcast_to(codes[r : r + 1, :], (COEF, COEF)).T
        own_box = code & (BOXES - 1)
        own_type = code >> 8
        lane = iota((COEF, COEF), 1)
        rows = pl.ds(r * COEF, COEF)
        member_t[rows, 0:COEF] = ones_where(own_box == lane)
        member_t[rows, COEF:BOXES] = ones_where(own_box == lane + COEF)
        spot = own_type * 8 + ((own_box >> 7) & 1) * 2 + ((own_box >> 3) & 1)
        hot[rows, :] = ones_where(spot == (lane & 63))
        field[rows, :] = own_type

    load_top.wait()
    load_tmats.wait()
    every = jnp.concatenate([tmats[t] for t in range(NTYPE)], axis=1)
    every_high, every_low = split(every)
    top_high, top_low = split(top[...])
    top_t[0], top_t[1] = split(dot(top_high, every_high) + dot(top_low, every_high) + dot(top_high, every_low))
    every3 = jnp.concatenate([every_high, every_high, every_low], axis=0)

    load_offsets.wait()
    load_near.wait()
    for copy in halo:
        copy.wait_recv()
    crossings = []
    row_cross = {-1: jnp.where(gx == 0, -1.0, 0.0), 0: 0.0, 1: jnp.where(gx == nx - 1, 1.0, 0.0)}
    col_cross = {-1: jnp.where(gy == 0, -1.0, 0.0), 0: 0.0, 1: jnp.where(gy == ny - 1, 1.0, 0.0)}
    angle = jnp.zeros((8, COEF), f32)
    for i, side in enumerate(sides):
        value = row_cross[side[0]] * theta[0] + col_cross[side[1]] * theta[1]
        angle = jnp.where(iota((8, COEF), 0) == i, value, angle)
    cosine, sine = jnp.cos(angle), jnp.sin(angle)

    def rotated(x, i):
        return cosine[i : i + 1] * x + sine[i : i + 1] * times_i(x)

    pad[0, 8 : 8 + LY, :] = rotated(rim[0], 0)
    pad[LX + 1, 8 : 8 + LY, :] = rotated(rim[1], 1)
    west, east = rotated(rim[2], 2), rotated(rim[3], 3)
    for x in range(LX):
        pad[x + 1, 7:8, :] = west[x : x + 1, :]
        pad[x + 1, 8 + LY : 9 + LY, :] = east[x : x + 1, :]
    for c, (x, y) in enumerate([(0, 7), (0, 8 + LY), (LX + 1, 7), (LX + 1, 8 + LY)]):
        pad[x, y : y + 1, :] = rotated(rim_corners[c], 4 + c)

    highs, lows, mats_high, mats_low = [], [], [], []
    for b in (-1, 0, 1):
        shifted = pad[:, 8 + b : 8 + b + LY, :].reshape((LX + 2) * LY, COEF)
        high, low = split(shifted)
        for a in (-1, 0, 1):
            entry = 0
            for o in range(NOFF):
                here = (offsets[0, o] == a) & (offsets[1, o] == b)
                entry = jnp.where(here, o, entry)
            mat_high, mat_low = split(near_mats[entry])
            start = (1 + a) * LY
            highs.append(high[start : start + BOXES])
            lows.append(low[start : start + BOXES])
            mats_high.append(mat_high)
            mats_low.append(mat_low)
    mat_high = jnp.concatenate(mats_high, axis=0)
    mats = jnp.concatenate([mat_high, jnp.concatenate(mats_low, axis=0)], axis=1)
    near2 = dot(jnp.concatenate(highs, axis=1), mats)
    near = near2[:, :COEF] + near2[:, COEF:] + dot(jnp.concatenate(lows, axis=1), mat_high)

    wait_all(ebuf, e_sem.at[1], planes - 1, 5)
    blocks = ebuf[...]
    sources = blocks.reshape(8 * planes, COEF)
    turned = pltpu.roll(times_i(sources), 4, 0)
    sources = jnp.where((iota(sources.shape, 0) & 4) == 0, sources, turned)
    source_high, source_low = split(sources)
    part2 = dot(far_w[0], jnp.concatenate([source_high, source_low], axis=1))
    part = part2[:, :COEF] + part2[:, COEF:] + dot(far_w[1], source_high)
    sample_sum = jnp.sum(blocks, axis=0)[4:5, :]
    for j in range(nz):
        pbuf[j, 0:4, :] = part[4 * j : 4 * j + 4]
        pbuf[j, 4:5, :] = sample_sum
    rbuf[z, 0:5, :] = pbuf[z, 0:5, :]
    for i in range(2):
        pl.semaphore_wait(met.at[i], 1)
    send_line(pbuf, rbuf, r_sem, 5, True)

    near_pair = jnp.concatenate(split(near), axis=1)
    for r in range(SD // CHUNK):
        rows = pl.ds(r * CHUNK, CHUNK)
        at2 = dot(member_t[rows, :], near_pair)
        at_high, at_low = split(at2[:, :COEF] + at2[:, COEF:])
        all_types = dot(jnp.concatenate([at_high, at_low, at_high], axis=1), every3)
        own_type = field[rows, :]
        value = all_types[:, :COEF]
        for t in range(1, NTYPE):
            value = jnp.where(own_type == t, all_types[:, t * COEF : (t + 1) * COEF], value)
        image[rows, :] = basis[KB - 1, rows, :] - value

    wait_all(rbuf, r_sem.at[1], nz - 1, 5)
    arrived = jnp.sum(rbuf[...], axis=0)
    far = jnp.where(iota((8, COEF), 0) < 4, arrived, 0.0)
    sample_row = arrived[4:5, :]
    far_high, far_low = split(far)
    far_pair = jnp.concatenate([far_high.astype(f32), far_low.astype(f32)], axis=0).astype(bf16)
    table2 = dot(far_pair, top_t[0]) + dot(far_pair, top_t[1])
    table = table2[0:8] + table2[8:16]
    table = jnp.concatenate([table[:, t * COEF : (t + 1) * COEF] for t in range(NTYPE)], axis=0)
    table = jnp.concatenate(split(table), axis=0)

    sample_count = float(nx * ny * SAMPLE * COEF)
    guess = [total_lane(sample_row, k) / sample_count for k in range(KB)]
    sums = [jnp.zeros((8, COEF), f32)] * (KB + 1)
    for r in range(SD // CHUNK):
        rows = pl.ds(r * CHUNK, CHUNK)
        w = image[rows, :] - dot(hot[rows, :], table)
        vectors = [basis[k, rows, :] for k in range(KB)]
        for k in range(KB):
            w = w - guess[k] * vectors[k]
        image[rows, :] = w
        for k in range(KB):
            sums[k] = sums[k] + fold(vectors[k] * w)
        sums[KB] = sums[KB] + fold(w * w)

    abuf[z, 0:1, :] = to_lanes(sums + grams)
    send_line(abuf, abuf, a_sem, 1, False)
    wait_all(abuf, a_sem.at[1], nz - 1, 1)
    bbuf[spot_in_plane, 0:1, :] = jnp.sum(abuf[...], axis=0)
    send_plane(bbuf, bbuf, b_sem, 1, False)
    wait_all(bbuf, b_sem.at[1], planes - 1, 1)
    totals = jnp.sum(bbuf[...], axis=0)
    inner = [total_lane(totals, k) for k in range(KB)]
    square = total_lane(totals, KB)
    gram, lane = {}, KB + 1
    for j in range(KB):
        for k in range(j, KB):
            gram[j, k] = gram[k, j] = total_lane(totals, lane)
            lane += 1
    coeffs = []
    for k in range(KB):
        value = inner[k]
        for j in range(KB):
            value = value + gram[k, j] * guess[j]
        coeffs.append(value / count)
    step = [coeffs[k] - guess[k] for k in range(KB)]
    for k in range(KB):
        along = -2.0 * inner[k]
        for j in range(KB):
            along = along + gram[k, j] * step[j]
        square = square + step[k] * along
    beta = jnp.sqrt(jnp.maximum(square, 0.0) / count + 1e-06)
    scale = 1.0 / beta

    for r in range(SD // CHUNK):
        rows = pl.ds(r * CHUNK, CHUNK)
        w = image[rows, :]
        for k in range(KB):
            w = w - step[k] * basis[k, rows, :]
        out_ref[rows, :] = w * scale
    for k, value in enumerate(coeffs + [beta]):
        hess_ref[k] = jnp.sum(value)
    for copy in halo:
        copy.wait_send()
    for buf, sem, number, rows in pending:
        wait_all(buf, sem.at[0], number, rows)


def on_device(nx, ny, basis, sphere_box, sphere_type, near_offsets, near_mats, up_mat, top_mat, tmats, bloch_angle):
    nz = nx // 2
    vmem, dma = pltpu.VMEM, pltpu.SemaphoreType.DMA
    return pl.pallas_call(
        functools.partial(kernel, nx, ny),
        out_shape=(pltpu.VMEM((SD, COEF), f32), pltpu.SMEM((KB + 1,), f32)),
        in_specs=[pl.BlockSpec(memory_space=pltpu.HBM)] * 9,
        out_specs=(pl.BlockSpec(memory_space=pltpu.VMEM), pl.BlockSpec(memory_space=pltpu.SMEM)),
        scratch_shapes=[
            vmem((KB, SD, COEF), f32),
            vmem((SD // COEF, COEF), i32),
            vmem((SD // COEF, COEF), i32),
            pltpu.SMEM((2, NOFF), i32),
            vmem((NOFF, COEF, COEF), f32),
            vmem((COEF, COEF), f32),
            vmem((COEF, COEF), f32),
            vmem((NTYPE, COEF, COEF), f32),
            pltpu.SMEM((2,), f32),
            vmem((2 * ny, 8, COEF), f32),
            vmem((nz, 8, COEF), f32),
            vmem((nz, 8, COEF), f32),
            vmem((nz, 1, COEF), f32),
            vmem((2 * ny, 1, COEF), f32),
            vmem((4, LX, COEF), f32),
            vmem((4, 1, COEF), f32),
            vmem((4, LX, COEF), f32),
            vmem((4, 1, COEF), f32),
            vmem((LX + 2, LY + 16, COEF), f32),
            vmem((2, 4 * nz, 16 * ny), bf16),
            vmem((2, COEF, NTYPE * COEF), bf16),
            vmem((SD, COEF), bf16),
            vmem((SD, BOXES), bf16),
            vmem((SD, COEF), f32),
            vmem((SD, COEF), i32),
            dma((11,)),
            dma((2,)),
            dma((2,)),
            dma((2,)),
            dma((2,)),
            dma((8,)),
            dma((8,)),
            pltpu.SemaphoreType.REGULAR((2,)),
        ],
        compiler_params=pltpu.CompilerParams(
            collective_id=0, has_side_effects=True, vmem_limit_bytes=48 * 1024 * 1024
        ),
        name="arnoldi_step",
    )(
        *[pltpu.with_memory_space_constraint(x, pltpu.HBM) for x in (basis,
        sphere_box.reshape(SD // COEF, COEF),
        sphere_type.reshape(SD // COEF, COEF),
        near_offsets.T, near_mats, up_mat, top_mat, tmats, bloch_angle)]
    )


def solution(mesh):
    return jax.shard_map(
        functools.partial(on_device, mesh.shape["gx"], mesh.shape["gy"]),
        mesh=mesh,
        in_specs=(
            P(None, ("gx", "gy"), None),
            P(("gx", "gy")),
            P(("gx", "gy")),
            P(),
            P(),
            P(),
            P(),
            P(),
            P(),
        ),
        out_specs=(P(("gx", "gy"), None), P()),
        check_vma=False,
    )
```

```python
import functools

import jax
import jax.numpy as jnp
from jax import lax
from jax.experimental import pallas as pl
from jax.experimental.pallas import tpu as pltpu
from jax.sharding import PartitionSpec as P

SD = 1024
LX = 16
LY = 16
KB = 3
COEF = 128
NTYPE = 8
NOFF = 9
BOXES = LX * LY
CHUNK = 256
SAMPLE = 128

MESH = pl.DeviceIdType.MESH
wave_number = 2.3
f32 = jnp.float32
bf16 = jnp.bfloat16
i32 = jnp.int32


def iota(shape, dim):
    return lax.broadcasted_iota(i32, shape, dim)


def split(x):
    high = x.astype(bf16)
    return high, (x - high.astype(f32)).astype(bf16)


def dot(a, b):
    return jnp.dot(a, b, preferred_element_type=f32)


def ones_where(mask):
    return jnp.where(mask, 1.0, 0.0).astype(bf16)


def times_i(x):
    turned = pltpu.roll(x, COEF // 2, x.ndim - 1)
    return jnp.where(iota(x.shape, x.ndim - 1) < COEF // 2, -turned, turned)


def total_lane(x, lane):
    return jnp.sum(jnp.where(iota(x.shape, 1) == lane, x, 0.0), axis=1, keepdims=True)


def to_lanes(parts, first=0):
    size = -(-len(parts) // 8) * 8
    rows = [jnp.sum(p, axis=0, keepdims=True) for p in parts]
    rows += [jnp.zeros((size - len(rows), COEF), f32)]
    sums = jnp.sum(jnp.concatenate(rows, axis=0), axis=1, keepdims=True)
    placed = jnp.where(iota((size, COEF), 0) + first == iota((size, COEF), 1), sums, 0.0)
    return jnp.sum(placed, axis=0, keepdims=True)


def fold(x):
    return jnp.sum(x.reshape(x.shape[0] // 8, 8, COEF), axis=0)


def far_weights(nx, ny, nz, gx, gy, theta):
    shape = (4 * nz, 16 * ny)
    m, n = iota(shape, 0), iota(shape, 1)
    grid_x, grid_y = 2 * nx, 2 * ny
    target_row = (gx // nz) * nz + (m >> 2)
    target_x, target_y = 2 * target_row + ((m >> 1) & 1), 2 * gy + (m & 1)
    source_row = jnp.where(n >= 8 * ny, nz, 0) + gx % nz
    source_x, source_y = 2 * source_row + ((n >> 1) & 1), 2 * ((n >> 3) & (ny - 1)) + (n & 1)
    shift_x = ((source_x - target_x + grid_x // 2) & (grid_x - 1)) - grid_x // 2
    shift_y = ((source_y - target_y + grid_y // 2) & (grid_y - 1)) - grid_y // 2
    wraps_x, wraps_y = target_x + shift_x - source_x, target_y + shift_y - source_y
    cross_x = jnp.where(wraps_x > 0, 1.0, jnp.where(wraps_x < 0, -1.0, 0.0))
    cross_y = jnp.where(wraps_y > 0, 1.0, jnp.where(wraps_y < 0, -1.0, 0.0))
    reach = jnp.maximum(jnp.abs(shift_x), jnp.abs(shift_y))
    distance = (shift_x * shift_x + shift_y * shift_y).astype(f32)
    radius = jnp.sqrt(jnp.maximum(distance, 1.0))
    weight = jnp.where(reach >= 2, 16.0 / radius, 0.0)
    angle = wave_number * radius + cross_x * theta[0] + cross_y * theta[1]
    return weight * jnp.where((n & 4) == 0, jnp.cos(angle), jnp.sin(angle))


def kernel(
    nx, ny,
    basis_in, box_in, type_in, offsets_in, near_in, up_in, top_in, tmats_in, bloch_in,
    out_ref, hess_ref,
    basis, box, kind, offsets, near_mats, up, top, tmats, bloch,
    ebuf, pbuf, rbuf, abuf, bbuf,
    edges, corners, rim, rim_corners, pad, far_w, top_t, hot, member_t, image, field,
    load_sem, e_sem, r_sem, a_sem, b_sem, h_send, h_recv, met,
):
    gx, gy = lax.axis_index("gx"), lax.axis_index("gy")
    nz = nx // 2
    planes = 2 * ny
    half, z = gx // nz, gx % nz
    spot_in_plane = half * ny + gy
    count = float(nx * ny * SD * COEF)

    def load(src, dst, i):
        copy = pltpu.make_async_copy(src, dst, load_sem.at[i])
        copy.start()
        return copy

    barrier = pltpu.get_barrier_semaphore()

    def in_line(k):
        return {"gx": half * nz + (z + k) % nz}

    def in_plane(k):
        peer = (spot_in_plane + k) % planes
        return peer, {"gx": (peer // ny) * nz + z, "gy": peer % ny}

    def greet_plane(k, c):
        pl.semaphore_signal(barrier, inc=1, device_id=in_plane(k)[1], device_id_type=MESH)
        return c

    reach = nz // 4
    for k in range(1, reach + 1):
        for way in (k, nz - k):
            pl.semaphore_signal(barrier, inc=1, device_id=in_line(way), device_id_type=MESH)
    lax.fori_loop(1, planes, greet_plane, 0)
    sides = [(-1, 0), (1, 0), (0, -1), (0, 1), (-1, -1), (-1, 1), (1, -1), (1, 1)]

    def beside(side):
        return {"gx": (gx + side[0] + nx) % nx, "gy": (gy + side[1] + ny) % ny}

    for side in sides[:2] + sides[4:]:
        pl.semaphore_signal(barrier, inc=1, device_id=beside(side), device_id_type=MESH)

    load_vec = load(basis_in.at[KB - 1], basis.at[KB - 1], 0)
    load_box = load(box_in, box, 1)
    load_up = load(up_in, up, 2)
    load_bloch = load(bloch_in, bloch, 3)
    others = pl.ds(0, KB - 1)
    load_sample = load(basis_in.at[others, pl.ds(0, SAMPLE)], basis.at[others, pl.ds(0, SAMPLE)], 4)
    load_type = load(type_in, kind, 5)
    load_offsets = load(offsets_in, offsets, 6)
    load_near = load(near_in, near_mats, 7)
    load_top = load(top_in, top, 8)
    load_tmats = load(tmats_in, tmats, 9)
    rest = pl.ds(SAMPLE, SD - SAMPLE)
    load_basis = load(basis_in.at[others, rest], basis.at[others, rest], 10)

    pending = []

    def send_line(src, dst, sem, rows, scatter):
        def body(k, c):
            far_half = nz // 2 + ((k + 1) // 2) * (1 - 2 * (k % 2))
            peer = (z + far_half) % nz
            pltpu.make_async_remote_copy(
                src.at[peer if scatter else z, pl.ds(0, rows)],
                dst.at[z, pl.ds(0, rows)],
                sem.at[0], sem.at[1], device_id=in_line(far_half), device_id_type=MESH,
            ).start()
            return c

        lax.fori_loop(0, nz - 1, body, 0)
        pending.append((src, sem, nz - 1, rows))

    def send_plane(src, dst, sem, rows, scatter):
        def body(k, c):
            peer, device = in_plane(k)
            pltpu.make_async_remote_copy(
                src.at[peer if scatter else spot_in_plane, pl.ds(0, rows)],
                dst.at[spot_in_plane, pl.ds(0, rows)],
                sem.at[0], sem.at[1], device_id=device, device_id_type=MESH,
            ).start()
            return c

        lax.fori_loop(1, planes, body, 0)
        pending.append((src, sem, planes - 1, rows))

    def wait_all(buf, sem, number, rows):
        span = buf.at[pl.ds(0, number), pl.ds(0, rows)]
        pltpu.make_async_copy(span, span, sem).wait()

    load_box.wait()
    boxes = box[...]
    quarters = ((boxes >> 7) & 1) * 2 + ((boxes >> 3) & 1)
    quarter_of = jnp.concatenate(
        [ones_where(iota((16, COEF), 0) == quarters[r : r + 1, :]) for r in range(SD // COEF)], axis=1
    )
    load_up.wait()
    up_high, up_low = split(up[...])
    load_vec.wait()
    vector_pair = jnp.concatenate(split(basis[KB - 1]), axis=1)
    quad2 = dot(quarter_of, vector_pair)
    quad_high, quad_low = split((quad2[:, :COEF] + quad2[:, COEF:])[0:8])
    pair = jnp.concatenate([quad_high.astype(f32), quad_low.astype(f32)], axis=0).astype(bf16)
    raised = dot(pair, up_high) + dot(pair, up_low)
    ebuf[spot_in_plane, 0:4, :] = (raised[0:8] + raised[8:16])[0:4]
    load_sample.wait()
    sampled = [basis[k, 0:SAMPLE, :] for k in range(KB)]
    ebuf[spot_in_plane, 4:5, :] = to_lanes([fold(v * sampled[KB - 1]) for v in sampled])
    pl.semaphore_wait(barrier, 2 * reach + planes - 1 + 6)
    send_plane(ebuf, ebuf, e_sem, 5, False)
    for i, way in enumerate((reach, nz - reach)):
        pl.semaphore_signal(met.at[i], inc=1, device_id=in_line(way), device_id_type=MESH)

    member = jnp.concatenate(
        [ones_where(iota((BOXES, COEF), 0) == boxes[r : r + 1, :]) for r in range(SD // COEF)], axis=1
    )
    leaf2 = dot(member, vector_pair)
    leaf = (leaf2[:, :COEF] + leaf2[:, COEF:]).reshape(LX, LY, COEF)

    edges[0] = leaf[0]
    edges[1] = leaf[LX - 1]
    edges[2] = leaf[:, 0, :]
    edges[3] = leaf[:, LY - 1, :]
    for c, (x, y) in enumerate([(0, 0), (0, LY - 1), (LX - 1, 0), (LX - 1, LY - 1)]):
        corners[c, 0:1, :] = leaf[x, y : y + 1, :]
    halo = []
    for i, side in enumerate(sides):
        other = sides.index((-side[0], -side[1]))
        if i < 4:
            src, dst = edges.at[i], rim.at[other]
        else:
            src, dst = corners.at[i - 4], rim_corners.at[other - 4]
        copy = pltpu.make_async_remote_copy(
            src, dst, h_send.at[i], h_recv.at[other], device_id=beside(side), device_id_type=MESH
        )
        copy.start()
        halo.append(copy)
    pad[1 : LX + 1, 8 : 8 + LY, :] = leaf

    load_bloch.wait()
    theta = (bloch[0], bloch[1])
    weights = far_weights(nx, ny, nz, gx, gy, theta)
    far_w[0], far_w[1] = split(weights)

    wait_all(ebuf, e_sem.at[1], planes - 1, 5)
    blocks = ebuf[...]
    sources = blocks.reshape(8 * planes, COEF)
    turned = pltpu.roll(times_i(sources), 4, 0)
    sources = jnp.where((iota(sources.shape, 0) & 4) == 0, sources, turned)
    source_high, source_low = split(sources)
    part2 = dot(far_w[0], jnp.concatenate([source_high, source_low], axis=1))
    part = part2[:, :COEF] + part2[:, COEF:] + dot(far_w[1], source_high)
    sample_sum = jnp.sum(blocks, axis=0)[4:5, :]
    for j in range(nz):
        pbuf[j, 0:4, :] = part[4 * j : 4 * j + 4]
        pbuf[j, 4:5, :] = sample_sum
    rbuf[z, 0:5, :] = pbuf[z, 0:5, :]
    for i in range(2):
        pl.semaphore_wait(met.at[i], 1)
    send_line(pbuf, rbuf, r_sem, 5, True)

    load_basis.wait()
    grams = []
    for j in range(KB):
        for k in range(j, KB):
            grams.append(fold(basis[j] * basis[k]))
    gram_lanes = to_lanes(grams, KB + 1)

    load_type.wait()
    codes = boxes + BOXES * kind[...]
    for r in range(SD // COEF):
        code = jnp.broadcast_to(codes[r : r + 1, :], (COEF, COEF)).T
        own_box = code & (BOXES - 1)
        own_type = code >> 8
        lane = iota((COEF, COEF), 1)
        rows = pl.ds(r * COEF, COEF)
        member_t[rows, 0:COEF] = ones_where(own_box == lane)
        member_t[rows, COEF:BOXES] = ones_where(own_box == lane + COEF)
        spot = own_type * 8 + ((own_box >> 7) & 1) * 2 + ((own_box >> 3) & 1)
        hot[rows, :] = ones_where(spot == (lane & 63))
        field[rows, :] = own_type

    load_top.wait()
    load_tmats.wait()
    every = jnp.concatenate([tmats[t] for t in range(NTYPE)], axis=1)
    every_high, every_low = split(every)
    top_high, top_low = split(top[...])
    top_t[0], top_t[1] = split(dot(top_high, every_high) + dot(top_low, every_high) + dot(top_high, every_low))
    every3 = jnp.concatenate([every_high, every_high, every_low], axis=0)

    load_offsets.wait()
    load_near.wait()
    for copy in halo:
        copy.wait_recv()
    crossings = []
    row_cross = {-1: jnp.where(gx == 0, -1.0, 0.0), 0: 0.0, 1: jnp.where(gx == nx - 1, 1.0, 0.0)}
    col_cross = {-1: jnp.where(gy == 0, -1.0, 0.0), 0: 0.0, 1: jnp.where(gy == ny - 1, 1.0, 0.0)}
    angle = jnp.zeros((8, COEF), f32)
    for i, side in enumerate(sides):
        value = row_cross[side[0]] * theta[0] + col_cross[side[1]] * theta[1]
        angle = jnp.where(iota((8, COEF), 0) == i, value, angle)
    cosine, sine = jnp.cos(angle), jnp.sin(angle)

    def rotated(x, i):
        return cosine[i : i + 1] * x + sine[i : i + 1] * times_i(x)

    pad[0, 8 : 8 + LY, :] = rotated(rim[0], 0)
    pad[LX + 1, 8 : 8 + LY, :] = rotated(rim[1], 1)
    west, east = rotated(rim[2], 2), rotated(rim[3], 3)
    for x in range(LX):
        pad[x + 1, 7:8, :] = west[x : x + 1, :]
        pad[x + 1, 8 + LY : 9 + LY, :] = east[x : x + 1, :]
    for c, (x, y) in enumerate([(0, 7), (0, 8 + LY), (LX + 1, 7), (LX + 1, 8 + LY)]):
        pad[x, y : y + 1, :] = rotated(rim_corners[c], 4 + c)

    highs, lows, mats_high, mats_low = [], [], [], []
    for b in (-1, 0, 1):
        shifted = pad[:, 8 + b : 8 + b + LY, :].reshape((LX + 2) * LY, COEF)
        high, low = split(shifted)
        for a in (-1, 0, 1):
            entry = 0
            for o in range(NOFF):
                here = (offsets[0, o] == a) & (offsets[1, o] == b)
                entry = jnp.where(here, o, entry)
            mat_high, mat_low = split(near_mats[entry])
            start = (1 + a) * LY
            highs.append(high[start : start + BOXES])
            lows.append(low[start : start + BOXES])
            mats_high.append(mat_high)
            mats_low.append(mat_low)
    mat_high = jnp.concatenate(mats_high, axis=0)
    mats = jnp.concatenate([mat_high, jnp.concatenate(mats_low, axis=0)], axis=1)
    near2 = dot(jnp.concatenate(highs, axis=1), mats)
    near = near2[:, :COEF] + near2[:, COEF:] + dot(jnp.concatenate(lows, axis=1), mat_high)

    near_pair = jnp.concatenate(split(near), axis=1)
    for r in range(SD // CHUNK):
        rows = pl.ds(r * CHUNK, CHUNK)
        at2 = dot(member_t[rows, :], near_pair)
        at_high, at_low = split(at2[:, :COEF] + at2[:, COEF:])
        all_types = dot(jnp.concatenate([at_high, at_low, at_high], axis=1), every3)
        own_type = field[rows, :]
        value = all_types[:, :COEF]
        for t in range(1, NTYPE):
            value = jnp.where(own_type == t, all_types[:, t * COEF : (t + 1) * COEF], value)
        image[rows, :] = basis[KB - 1, rows, :] - value

    wait_all(rbuf, r_sem.at[1], nz - 1, 5)
    arrived = jnp.sum(rbuf[...], axis=0)
    far = jnp.where(iota((8, COEF), 0) < 4, arrived, 0.0)
    sample_row = arrived[4:5, :]
    far_high, far_low = split(far)
    far_pair = jnp.concatenate([far_high.astype(f32), far_low.astype(f32)], axis=0).astype(bf16)
    table2 = dot(far_pair, top_t[0]) + dot(far_pair, top_t[1])
    table = table2[0:8] + table2[8:16]
    table = jnp.concatenate([table[:, t * COEF : (t + 1) * COEF] for t in range(NTYPE)], axis=0)
    table = jnp.concatenate(split(table), axis=0)

    sample_count = float(nx * ny * SAMPLE * COEF)
    guess = [total_lane(sample_row, k) / sample_count for k in range(KB)]
    sums = [jnp.zeros((8, COEF), f32)] * (KB + 1)
    for r in range(SD // CHUNK):
        rows = pl.ds(r * CHUNK, CHUNK)
        w = image[rows, :] - dot(hot[rows, :], table)
        vectors = [basis[k, rows, :] for k in range(KB)]
        for k in range(KB):
            w = w - guess[k] * vectors[k]
        image[rows, :] = w
        for k in range(KB):
            sums[k] = sums[k] + fold(vectors[k] * w)
        sums[KB] = sums[KB] + fold(w * w)

    bbuf[spot_in_plane, 0:1, :] = to_lanes(sums) + gram_lanes
    send_plane(bbuf, bbuf, b_sem, 1, False)
    wait_all(bbuf, b_sem.at[1], planes - 1, 1)
    abuf[z, 0:1, :] = jnp.sum(bbuf[...], axis=0)
    send_line(abuf, abuf, a_sem, 1, False)
    wait_all(abuf, a_sem.at[1], nz - 1, 1)
    totals = jnp.sum(abuf[...], axis=0)
    inner = [total_lane(totals, k) for k in range(KB)]
    square = total_lane(totals, KB)
    gram, lane = {}, KB + 1
    for j in range(KB):
        for k in range(j, KB):
            gram[j, k] = gram[k, j] = total_lane(totals, lane)
            lane += 1
    coeffs = []
    for k in range(KB):
        value = inner[k]
        for j in range(KB):
            value = value + gram[k, j] * guess[j]
        coeffs.append(value / count)
    step = [coeffs[k] - guess[k] for k in range(KB)]
    for k in range(KB):
        along = -2.0 * inner[k]
        for j in range(KB):
            along = along + gram[k, j] * step[j]
        square = square + step[k] * along
    beta = jnp.sqrt(jnp.maximum(square, 0.0) / count + 1e-06)
    scale = 1.0 / beta

    for r in range(SD // CHUNK):
        rows = pl.ds(r * CHUNK, CHUNK)
        w = image[rows, :]
        for k in range(KB):
            w = w - step[k] * basis[k, rows, :]
        out_ref[rows, :] = w * scale
    for k, value in enumerate(coeffs + [beta]):
        hess_ref[k] = jnp.sum(value)
    for copy in halo:
        copy.wait_send()
    for buf, sem, number, rows in pending:
        wait_all(buf, sem.at[0], number, rows)


def on_device(nx, ny, basis, sphere_box, sphere_type, near_offsets, near_mats, up_mat, top_mat, tmats, bloch_angle):
    nz = nx // 2
    vmem, dma = pltpu.VMEM, pltpu.SemaphoreType.DMA
    return pl.pallas_call(
        functools.partial(kernel, nx, ny),
        out_shape=(pltpu.VMEM((SD, COEF), f32), pltpu.SMEM((KB + 1,), f32)),
        in_specs=[pl.BlockSpec(memory_space=pltpu.HBM)] * 9,
        out_specs=(pl.BlockSpec(memory_space=pltpu.VMEM), pl.BlockSpec(memory_space=pltpu.SMEM)),
        scratch_shapes=[
            vmem((KB, SD, COEF), f32),
            vmem((SD // COEF, COEF), i32),
            vmem((SD // COEF, COEF), i32),
            pltpu.SMEM((2, NOFF), i32),
            vmem((NOFF, COEF, COEF), f32),
            vmem((COEF, COEF), f32),
            vmem((COEF, COEF), f32),
            vmem((NTYPE, COEF, COEF), f32),
            pltpu.SMEM((2,), f32),
            vmem((2 * ny, 8, COEF), f32),
            vmem((nz, 8, COEF), f32),
            vmem((nz, 8, COEF), f32),
            vmem((nz, 1, COEF), f32),
            vmem((2 * ny, 1, COEF), f32),
            vmem((4, LX, COEF), f32),
            vmem((4, 1, COEF), f32),
            vmem((4, LX, COEF), f32),
            vmem((4, 1, COEF), f32),
            vmem((LX + 2, LY + 16, COEF), f32),
            vmem((2, 4 * nz, 16 * ny), bf16),
            vmem((2, COEF, NTYPE * COEF), bf16),
            vmem((SD, COEF), bf16),
            vmem((SD, BOXES), bf16),
            vmem((SD, COEF), f32),
            vmem((SD, COEF), i32),
            dma((11,)),
            dma((2,)),
            dma((2,)),
            dma((2,)),
            dma((2,)),
            dma((8,)),
            dma((8,)),
            pltpu.SemaphoreType.REGULAR((2,)),
        ],
        compiler_params=pltpu.CompilerParams(
            collective_id=0, has_side_effects=True, vmem_limit_bytes=48 * 1024 * 1024
        ),
        name="arnoldi_step",
    )(
        *[pltpu.with_memory_space_constraint(x, pltpu.HBM) for x in (basis,
        sphere_box.reshape(SD // COEF, COEF),
        sphere_type.reshape(SD // COEF, COEF),
        near_offsets.T, near_mats, up_mat, top_mat, tmats, bloch_angle)]
    )


def solution(mesh):
    return jax.shard_map(
        functools.partial(on_device, mesh.shape["gx"], mesh.shape["gy"]),
        mesh=mesh,
        in_specs=(
            P(None, ("gx", "gy"), None),
            P(("gx", "gy")),
            P(("gx", "gy")),
            P(),
            P(),
            P(),
            P(),
            P(),
            P(),
        ),
        out_specs=(P(("gx", "gy"), None), P()),
        check_vma=False,
    )
```

```python
import functools

import jax
import jax.numpy as jnp
from jax import lax
from jax.experimental import pallas as pl
from jax.experimental.pallas import tpu as pltpu
from jax.sharding import PartitionSpec as P

SD = 1024
LX = 16
LY = 16
KB = 3
COEF = 128
NTYPE = 8
NOFF = 9
BOXES = LX * LY
CHUNK = 256

MESH = pl.DeviceIdType.MESH
wave_number = 2.3
f32 = jnp.float32
bf16 = jnp.bfloat16
i32 = jnp.int32


def iota(shape, dim):
    return lax.broadcasted_iota(i32, shape, dim)


def split(x):
    high = x.astype(bf16)
    return high, (x - high.astype(f32)).astype(bf16)


def dot(a, b):
    return jnp.dot(a, b, preferred_element_type=f32)


def ones_where(mask):
    return jnp.where(mask, 1.0, 0.0).astype(bf16)


def times_i(x):
    turned = pltpu.roll(x, COEF // 2, x.ndim - 1)
    return jnp.where(iota(x.shape, x.ndim - 1) < COEF // 2, -turned, turned)


def total_lane(x, lane):
    return jnp.sum(jnp.where(iota(x.shape, 1) == lane, x, 0.0), axis=1, keepdims=True)


def to_lanes(parts, first=0):
    size = -(-len(parts) // 8) * 8
    rows = [jnp.sum(p, axis=0, keepdims=True) for p in parts]
    rows += [jnp.zeros((size - len(rows), COEF), f32)]
    sums = jnp.sum(jnp.concatenate(rows, axis=0), axis=1, keepdims=True)
    placed = jnp.where(iota((size, COEF), 0) + first == iota((size, COEF), 1), sums, 0.0)
    return jnp.sum(placed, axis=0, keepdims=True)


def fold(x):
    return jnp.sum(x.reshape(x.shape[0] // 8, 8, COEF), axis=0)


def far_weights(nx, ny, nz, gx, gy, theta):
    shape = (4 * nz, 16 * ny)
    m, n = iota(shape, 0), iota(shape, 1)
    grid_x, grid_y = 2 * nx, 2 * ny
    target_row = (gx // nz) * nz + (m >> 2)
    target_x, target_y = 2 * target_row + ((m >> 1) & 1), 2 * gy + (m & 1)
    source_row = jnp.where(n >= 8 * ny, nz, 0) + gx % nz
    source_x, source_y = 2 * source_row + ((n >> 1) & 1), 2 * ((n >> 3) & (ny - 1)) + (n & 1)
    shift_x = ((source_x - target_x + grid_x // 2) & (grid_x - 1)) - grid_x // 2
    shift_y = ((source_y - target_y + grid_y // 2) & (grid_y - 1)) - grid_y // 2
    wraps_x, wraps_y = target_x + shift_x - source_x, target_y + shift_y - source_y
    cross_x = jnp.where(wraps_x > 0, 1.0, jnp.where(wraps_x < 0, -1.0, 0.0))
    cross_y = jnp.where(wraps_y > 0, 1.0, jnp.where(wraps_y < 0, -1.0, 0.0))
    reach = jnp.maximum(jnp.abs(shift_x), jnp.abs(shift_y))
    distance = (shift_x * shift_x + shift_y * shift_y).astype(f32)
    radius = jnp.sqrt(jnp.maximum(distance, 1.0))
    weight = jnp.where(reach >= 2, 16.0 / radius, 0.0)
    angle = wave_number * radius + cross_x * theta[0] + cross_y * theta[1]
    return weight * jnp.where((n & 4) == 0, jnp.cos(angle), jnp.sin(angle))


def kernel(
    nx, ny,
    basis_in, box_in, type_in, offsets_in, near_in, up_in, top_in, tmats_in, bloch_in,
    out_ref, hess_ref,
    basis, box, kind, offsets, near_mats, up, top, tmats, bloch,
    ebuf, pbuf, rbuf, abuf, bbuf,
    edges, corners, rim, rim_corners, pad, far_w, top_t, hot, member_t, image, field,
    load_sem, e_sem, r_sem, a_sem, b_sem, h_send, h_recv, met,
):
    gx, gy = lax.axis_index("gx"), lax.axis_index("gy")
    nz = nx // 2
    planes = 2 * ny
    half, z = gx // nz, gx % nz
    spot_in_plane = half * ny + gy
    count = float(nx * ny * SD * COEF)

    def load(src, dst, i):
        copy = pltpu.make_async_copy(src, dst, load_sem.at[i])
        copy.start()
        return copy

    barrier = pltpu.get_barrier_semaphore()

    def in_line(k):
        return {"gx": half * nz + (z + k) % nz}

    def in_plane(k):
        peer = (spot_in_plane + k) % planes
        return peer, {"gx": (peer // ny) * nz + z, "gy": peer % ny}

    def greet_plane(k, c):
        pl.semaphore_signal(barrier, inc=1, device_id=in_plane(k)[1], device_id_type=MESH)
        return c

    reach = nz // 4
    for k in range(1, reach + 1):
        for way in (k, nz - k):
            pl.semaphore_signal(barrier, inc=1, device_id=in_line(way), device_id_type=MESH)
    lax.fori_loop(1, planes, greet_plane, 0)
    sides = [(-1, 0), (1, 0), (0, -1), (0, 1), (-1, -1), (-1, 1), (1, -1), (1, 1)]

    def beside(side):
        return {"gx": (gx + side[0] + nx) % nx, "gy": (gy + side[1] + ny) % ny}

    for side in sides[:2] + sides[4:]:
        pl.semaphore_signal(barrier, inc=1, device_id=beside(side), device_id_type=MESH)

    load_vec = load(basis_in.at[KB - 1], basis.at[KB - 1], 0)
    load_box = load(box_in, box, 1)
    load_up = load(up_in, up, 2)
    load_bloch = load(bloch_in, bloch, 3)
    others = pl.ds(0, KB - 1)
    load_basis = load(basis_in.at[others], basis.at[others], 4)
    load_type = load(type_in, kind, 5)
    load_offsets = load(offsets_in, offsets, 6)
    load_near = load(near_in, near_mats, 7)
    load_top = load(top_in, top, 8)
    load_tmats = load(tmats_in, tmats, 9)

    pending = []

    def send_line(src, dst, sem, rows, scatter):
        def body(k, c):
            far_half = nz // 2 + ((k + 1) // 2) * (1 - 2 * (k % 2))
            peer = (z + far_half) % nz
            pltpu.make_async_remote_copy(
                src.at[peer if scatter else z, pl.ds(0, rows)],
                dst.at[z, pl.ds(0, rows)],
                sem.at[0], sem.at[1], device_id=in_line(far_half), device_id_type=MESH,
            ).start()
            return c

        lax.fori_loop(0, nz - 1, body, 0)
        pending.append((src, sem, nz - 1, rows))

    def send_plane(src, dst, sem, rows, scatter):
        def body(k, c):
            peer, device = in_plane(k)
            pltpu.make_async_remote_copy(
                src.at[peer if scatter else spot_in_plane, pl.ds(0, rows)],
                dst.at[spot_in_plane, pl.ds(0, rows)],
                sem.at[0], sem.at[1], device_id=device, device_id_type=MESH,
            ).start()
            return c

        lax.fori_loop(1, planes, body, 0)
        pending.append((src, sem, planes - 1, rows))

    def wait_all(buf, sem, number, rows):
        span = buf.at[pl.ds(0, number), pl.ds(0, rows)]
        pltpu.make_async_copy(span, span, sem).wait()

    load_box.wait()
    boxes = box[...]
    quarters = ((boxes >> 7) & 1) * 2 + ((boxes >> 3) & 1)
    quarter_of = jnp.concatenate(
        [ones_where(iota((16, COEF), 0) == quarters[r : r + 1, :]) for r in range(SD // COEF)], axis=1
    )
    load_up.wait()
    up_high, up_low = split(up[...])
    load_vec.wait()
    vector_pair = jnp.concatenate(split(basis[KB - 1]), axis=1)
    quad2 = dot(quarter_of, vector_pair)
    quad_high, quad_low = split((quad2[:, :COEF] + quad2[:, COEF:])[0:8])
    pair = jnp.concatenate([quad_high.astype(f32), quad_low.astype(f32)], axis=0).astype(bf16)
    raised = dot(pair, up_high) + dot(pair, up_low)
    ebuf[spot_in_plane, 0:4, :] = (raised[0:8] + raised[8:16])[0:4]
    pl.semaphore_wait(barrier, 2 * reach + planes - 1 + 6)
    send_plane(ebuf, ebuf, e_sem, 4, False)
    for i, way in enumerate((reach, nz - reach)):
        pl.semaphore_signal(met.at[i], inc=1, device_id=in_line(way), device_id_type=MESH)

    member = jnp.concatenate(
        [ones_where(iota((BOXES, COEF), 0) == boxes[r : r + 1, :]) for r in range(SD // COEF)], axis=1
    )
    leaf2 = dot(member, vector_pair)
    leaf = (leaf2[:, :COEF] + leaf2[:, COEF:]).reshape(LX, LY, COEF)

    edges[0] = leaf[0]
    edges[1] = leaf[LX - 1]
    edges[2] = leaf[:, 0, :]
    edges[3] = leaf[:, LY - 1, :]
    for c, (x, y) in enumerate([(0, 0), (0, LY - 1), (LX - 1, 0), (LX - 1, LY - 1)]):
        corners[c, 0:1, :] = leaf[x, y : y + 1, :]
    halo = []
    for i, side in enumerate(sides):
        other = sides.index((-side[0], -side[1]))
        if i < 4:
            src, dst = edges.at[i], rim.at[other]
        else:
            src, dst = corners.at[i - 4], rim_corners.at[other - 4]
        copy = pltpu.make_async_remote_copy(
            src, dst, h_send.at[i], h_recv.at[other], device_id=beside(side), device_id_type=MESH
        )
        copy.start()
        halo.append(copy)
    pad[1 : LX + 1, 8 : 8 + LY, :] = leaf

    load_bloch.wait()
    theta = (bloch[0], bloch[1])
    weights = far_weights(nx, ny, nz, gx, gy, theta)
    far_w[0], far_w[1] = split(weights)

    wait_all(ebuf, e_sem.at[1], planes - 1, 4)
    sources = ebuf[...].reshape(8 * planes, COEF)
    turned = pltpu.roll(times_i(sources), 4, 0)
    sources = jnp.where((iota(sources.shape, 0) & 4) == 0, sources, turned)
    source_high, source_low = split(sources)
    part2 = dot(far_w[0], jnp.concatenate([source_high, source_low], axis=1))
    part = part2[:, :COEF] + part2[:, COEF:] + dot(far_w[1], source_high)
    for j in range(nz):
        pbuf[j, 0:4, :] = part[4 * j : 4 * j + 4]
    rbuf[z, 0:4, :] = pbuf[z, 0:4, :]
    for i in range(2):
        pl.semaphore_wait(met.at[i], 1)
    send_line(pbuf, rbuf, r_sem, 4, True)

    load_basis.wait()
    grams = []
    for j in range(KB):
        for k in range(j, KB):
            grams.append(fold(basis[j] * basis[k]))
    gram_lanes = to_lanes(grams, KB + 1)

    load_type.wait()
    codes = boxes + BOXES * kind[...]
    for r in range(SD // COEF):
        code = jnp.broadcast_to(codes[r : r + 1, :], (COEF, COEF)).T
        own_box = code & (BOXES - 1)
        own_type = code >> 8
        lane = iota((COEF, COEF), 1)
        rows = pl.ds(r * COEF, COEF)
        member_t[rows, 0:COEF] = ones_where(own_box == lane)
        member_t[rows, COEF:BOXES] = ones_where(own_box == lane + COEF)
        spot = own_type * 8 + ((own_box >> 7) & 1) * 2 + ((own_box >> 3) & 1)
        hot[rows, :] = ones_where(spot == (lane & 63))
        field[rows, :] = own_type

    spots = kind[...] * 8 + quarters
    hot_t = jnp.concatenate(
        [ones_where(iota((8 * NTYPE, COEF), 0) == spots[r : r + 1, :]) for r in range(SD // COEF)], axis=1
    )
    numbers = jnp.sum(hot_t.astype(f32), axis=1, keepdims=True)

    def class_sums(x):
        both = dot(hot_t, jnp.concatenate(split(x), axis=1))
        return both[:, :COEF] + both[:, COEF:]

    basis_sums = [class_sums(basis[k]) for k in range(KB)]

    load_top.wait()
    load_tmats.wait()
    every = jnp.concatenate([tmats[t] for t in range(NTYPE)], axis=1)
    every_high, every_low = split(every)
    top_high, top_low = split(top[...])
    top_t[0], top_t[1] = split(dot(top_high, every_high) + dot(top_low, every_high) + dot(top_high, every_low))
    every3 = jnp.concatenate([every_high, every_high, every_low], axis=0)

    load_offsets.wait()
    load_near.wait()
    for copy in halo:
        copy.wait_recv()
    crossings = []
    row_cross = {-1: jnp.where(gx == 0, -1.0, 0.0), 0: 0.0, 1: jnp.where(gx == nx - 1, 1.0, 0.0)}
    col_cross = {-1: jnp.where(gy == 0, -1.0, 0.0), 0: 0.0, 1: jnp.where(gy == ny - 1, 1.0, 0.0)}
    angle = jnp.zeros((8, COEF), f32)
    for i, side in enumerate(sides):
        value = row_cross[side[0]] * theta[0] + col_cross[side[1]] * theta[1]
        angle = jnp.where(iota((8, COEF), 0) == i, value, angle)
    cosine, sine = jnp.cos(angle), jnp.sin(angle)

    def rotated(x, i):
        return cosine[i : i + 1] * x + sine[i : i + 1] * times_i(x)

    pad[0, 8 : 8 + LY, :] = rotated(rim[0], 0)
    pad[LX + 1, 8 : 8 + LY, :] = rotated(rim[1], 1)
    west, east = rotated(rim[2], 2), rotated(rim[3], 3)
    for x in range(LX):
        pad[x + 1, 7:8, :] = west[x : x + 1, :]
        pad[x + 1, 8 + LY : 9 + LY, :] = east[x : x + 1, :]
    for c, (x, y) in enumerate([(0, 7), (0, 8 + LY), (LX + 1, 7), (LX + 1, 8 + LY)]):
        pad[x, y : y + 1, :] = rotated(rim_corners[c], 4 + c)

    highs, lows, mats_high, mats_low = [], [], [], []
    for b in (-1, 0, 1):
        shifted = pad[:, 8 + b : 8 + b + LY, :].reshape((LX + 2) * LY, COEF)
        high, low = split(shifted)
        for a in (-1, 0, 1):
            entry = 0
            for o in range(NOFF):
                here = (offsets[0, o] == a) & (offsets[1, o] == b)
                entry = jnp.where(here, o, entry)
            mat_high, mat_low = split(near_mats[entry])
            start = (1 + a) * LY
            highs.append(high[start : start + BOXES])
            lows.append(low[start : start + BOXES])
            mats_high.append(mat_high)
            mats_low.append(mat_low)
    mat_high = jnp.concatenate(mats_high, axis=0)
    mats = jnp.concatenate([mat_high, jnp.concatenate(mats_low, axis=0)], axis=1)
    near2 = dot(jnp.concatenate(highs, axis=1), mats)
    near = near2[:, :COEF] + near2[:, COEF:] + dot(jnp.concatenate(lows, axis=1), mat_high)

    near_pair = jnp.concatenate(split(near), axis=1)
    for r in range(SD // CHUNK):
        rows = pl.ds(r * CHUNK, CHUNK)
        at2 = dot(member_t[rows, :], near_pair)
        at_high, at_low = split(at2[:, :COEF] + at2[:, COEF:])
        all_types = dot(jnp.concatenate([at_high, at_low, at_high], axis=1), every3)
        own_type = field[rows, :]
        value = all_types[:, :COEF]
        for t in range(1, NTYPE):
            value = jnp.where(own_type == t, all_types[:, t * COEF : (t + 1) * COEF], value)
        image[rows, :] = -value

    near_sums = [fold(basis[k] * image[...]) for k in range(KB)] + [fold(image[...] * image[...])]
    near_class = class_sums(image[...])

    wait_all(rbuf, r_sem.at[1], nz - 1, 4)
    arrived = jnp.sum(rbuf[...], axis=0)
    far = jnp.where(iota((8, COEF), 0) < 4, arrived, 0.0)
    far_high, far_low = split(far)
    far_pair = jnp.concatenate([far_high.astype(f32), far_low.astype(f32)], axis=0).astype(bf16)
    table2 = dot(far_pair, top_t[0]) + dot(far_pair, top_t[1])
    table = table2[0:8] + table2[8:16]
    table = jnp.concatenate([table[:, t * COEF : (t + 1) * COEF] for t in range(NTYPE)], axis=0)
    sums = [near_sums[k] - fold(table * basis_sums[k]) for k in range(KB)]
    sums.append(near_sums[KB] + fold(table * (table * numbers - 2.0 * near_class)))

    bbuf[spot_in_plane, 0:1, :] = to_lanes(sums) + gram_lanes
    send_plane(bbuf, bbuf, b_sem, 1, False)
    table = jnp.concatenate(split(table), axis=0)
    for r in range(SD // CHUNK):
        rows = pl.ds(r * CHUNK, CHUNK)
        image[rows, :] = image[rows, :] - dot(hot[rows, :], table)
    wait_all(bbuf, b_sem.at[1], planes - 1, 1)
    abuf[z, 0:1, :] = jnp.sum(bbuf[...], axis=0)
    send_line(abuf, abuf, a_sem, 1, False)
    wait_all(abuf, a_sem.at[1], nz - 1, 1)
    totals = jnp.sum(abuf[...], axis=0)
    inner = [total_lane(totals, k) for k in range(KB)]
    square = total_lane(totals, KB)
    gram, lane = {}, KB + 1
    for j in range(KB):
        for k in range(j, KB):
            gram[j, k] = gram[k, j] = total_lane(totals, lane)
            lane += 1
    coeffs = [(inner[k] + gram[k, KB - 1]) / count for k in range(KB)]
    step = [coeffs[k] - (1.0 if k == KB - 1 else 0.0) for k in range(KB)]
    for k in range(KB):
        along = -2.0 * inner[k]
        for j in range(KB):
            along = along + gram[k, j] * step[j]
        square = square + step[k] * along
    beta = jnp.sqrt(jnp.maximum(square, 0.0) / count + 1e-06)
    scale = 1.0 / beta

    for r in range(SD // CHUNK):
        rows = pl.ds(r * CHUNK, CHUNK)
        w = image[rows, :]
        for k in range(KB):
            w = w - step[k] * basis[k, rows, :]
        out_ref[rows, :] = w * scale
    for k, value in enumerate(coeffs + [beta]):
        hess_ref[k] = jnp.sum(value)
    for copy in halo:
        copy.wait_send()
    for buf, sem, number, rows in pending:
        wait_all(buf, sem.at[0], number, rows)


def on_device(nx, ny, basis, sphere_box, sphere_type, near_offsets, near_mats, up_mat, top_mat, tmats, bloch_angle):
    nz = nx // 2
    vmem, dma = pltpu.VMEM, pltpu.SemaphoreType.DMA
    return pl.pallas_call(
        functools.partial(kernel, nx, ny),
        out_shape=(pltpu.VMEM((SD, COEF), f32), pltpu.SMEM((KB + 1,), f32)),
        in_specs=[pl.BlockSpec(memory_space=pltpu.HBM)] * 9,
        out_specs=(pl.BlockSpec(memory_space=pltpu.VMEM), pl.BlockSpec(memory_space=pltpu.SMEM)),
        scratch_shapes=[
            vmem((KB, SD, COEF), f32),
            vmem((SD // COEF, COEF), i32),
            vmem((SD // COEF, COEF), i32),
            pltpu.SMEM((2, NOFF), i32),
            vmem((NOFF, COEF, COEF), f32),
            vmem((COEF, COEF), f32),
            vmem((COEF, COEF), f32),
            vmem((NTYPE, COEF, COEF), f32),
            pltpu.SMEM((2,), f32),
            vmem((2 * ny, 8, COEF), f32),
            vmem((nz, 8, COEF), f32),
            vmem((nz, 8, COEF), f32),
            vmem((nz, 1, COEF), f32),
            vmem((2 * ny, 1, COEF), f32),
            vmem((4, LX, COEF), f32),
            vmem((4, 1, COEF), f32),
            vmem((4, LX, COEF), f32),
            vmem((4, 1, COEF), f32),
            vmem((LX + 2, LY + 16, COEF), f32),
            vmem((2, 4 * nz, 16 * ny), bf16),
            vmem((2, COEF, NTYPE * COEF), bf16),
            vmem((SD, COEF), bf16),
            vmem((SD, BOXES), bf16),
            vmem((SD, COEF), f32),
            vmem((SD, COEF), i32),
            dma((10,)),
            dma((2,)),
            dma((2,)),
            dma((2,)),
            dma((2,)),
            dma((8,)),
            dma((8,)),
            pltpu.SemaphoreType.REGULAR((2,)),
        ],
        compiler_params=pltpu.CompilerParams(
            collective_id=0, has_side_effects=True, vmem_limit_bytes=48 * 1024 * 1024
        ),
        name="arnoldi_step",
    )(
        *[pltpu.with_memory_space_constraint(x, pltpu.HBM) for x in (basis,
        sphere_box.reshape(SD // COEF, COEF),
        sphere_type.reshape(SD // COEF, COEF),
        near_offsets.T, near_mats, up_mat, top_mat, tmats, bloch_angle)]
    )


def solution(mesh):
    return jax.shard_map(
        functools.partial(on_device, mesh.shape["gx"], mesh.shape["gy"]),
        mesh=mesh,
        in_specs=(
            P(None, ("gx", "gy"), None),
            P(("gx", "gy")),
            P(("gx", "gy")),
            P(),
            P(),
            P(),
            P(),
            P(),
            P(),
        ),
        out_specs=(P(("gx", "gy"), None), P()),
        check_vma=False,
    )
```

```python
import functools

import jax
import jax.numpy as jnp
from jax import lax
from jax.experimental import pallas as pl
from jax.experimental.pallas import tpu as pltpu
from jax.sharding import PartitionSpec as P

SD = 1024
LX = 16
LY = 16
KB = 3
COEF = 128
NTYPE = 8
NOFF = 9
BOXES = LX * LY
CHUNK = 256

MESH = pl.DeviceIdType.MESH
wave_number = 2.3
f32 = jnp.float32
bf16 = jnp.bfloat16
i32 = jnp.int32


def iota(shape, dim):
    return lax.broadcasted_iota(i32, shape, dim)


def split(x):
    high = x.astype(bf16)
    return high, (x - high.astype(f32)).astype(bf16)


def dot(a, b):
    return jnp.dot(a, b, preferred_element_type=f32)


def ones_where(mask):
    return jnp.where(mask, 1.0, 0.0).astype(bf16)


def times_i(x):
    turned = pltpu.roll(x, COEF // 2, x.ndim - 1)
    return jnp.where(iota(x.shape, x.ndim - 1) < COEF // 2, -turned, turned)


def total_lane(x, lane):
    return jnp.sum(jnp.where(iota(x.shape, 1) == lane, x, 0.0), axis=1, keepdims=True)


def to_lanes(parts, first=0):
    size = -(-len(parts) // 8) * 8
    rows = [jnp.sum(p, axis=0, keepdims=True) for p in parts]
    rows += [jnp.zeros((size - len(rows), COEF), f32)]
    sums = jnp.sum(jnp.concatenate(rows, axis=0), axis=1, keepdims=True)
    placed = jnp.where(iota((size, COEF), 0) + first == iota((size, COEF), 1), sums, 0.0)
    return jnp.sum(placed, axis=0, keepdims=True)


def fold(x):
    return jnp.sum(x.reshape(x.shape[0] // 8, 8, COEF), axis=0)


def far_weights(nx, ny, nz, gx, gy, theta):
    shape = (4 * nz, 16 * ny)
    m, n = iota(shape, 0), iota(shape, 1)
    grid_x, grid_y = 2 * nx, 2 * ny
    target_row = (gx // nz) * nz + (m >> 2)
    target_x, target_y = 2 * target_row + ((m >> 1) & 1), 2 * gy + (m & 1)
    source_row = jnp.where(n >= 8 * ny, nz, 0) + gx % nz
    source_x, source_y = 2 * source_row + ((n >> 1) & 1), 2 * ((n >> 3) & (ny - 1)) + (n & 1)
    shift_x = ((source_x - target_x + grid_x // 2) & (grid_x - 1)) - grid_x // 2
    shift_y = ((source_y - target_y + grid_y // 2) & (grid_y - 1)) - grid_y // 2
    wraps_x, wraps_y = target_x + shift_x - source_x, target_y + shift_y - source_y
    cross_x = jnp.where(wraps_x > 0, 1.0, jnp.where(wraps_x < 0, -1.0, 0.0))
    cross_y = jnp.where(wraps_y > 0, 1.0, jnp.where(wraps_y < 0, -1.0, 0.0))
    reach = jnp.maximum(jnp.abs(shift_x), jnp.abs(shift_y))
    distance = (shift_x * shift_x + shift_y * shift_y).astype(f32)
    radius = jnp.sqrt(jnp.maximum(distance, 1.0))
    weight = jnp.where(reach >= 2, 16.0 / radius, 0.0)
    angle = wave_number * radius + cross_x * theta[0] + cross_y * theta[1]
    return weight * jnp.where((n & 4) == 0, jnp.cos(angle), jnp.sin(angle))


def kernel(
    nx, ny,
    basis_in, box_in, type_in, offsets_in, near_in, up_in, top_in, tmats_in, bloch_in,
    out_ref, hess_ref,
    basis, box, kind, offsets, near_mats, up, top, tmats, bloch,
    ebuf, pbuf, rbuf, abuf, bbuf,
    edges, corners, rim, rim_corners, pad, far_w, top_t, hot, member_t, image, field,
    load_sem, e_sem, r_sem, a_sem, b_sem, h_send, h_recv, met,
):
    gx, gy = lax.axis_index("gx"), lax.axis_index("gy")
    nz = nx // 2
    planes = 2 * ny
    half, z = gx // nz, gx % nz
    spot_in_plane = half * ny + gy
    count = float(nx * ny * SD * COEF)

    def load(src, dst, i):
        copy = pltpu.make_async_copy(src, dst, load_sem.at[i])
        copy.start()
        return copy

    barrier = pltpu.get_barrier_semaphore()

    def in_line(k):
        return {"gx": half * nz + (z + k) % nz}

    def in_plane(k):
        peer = (spot_in_plane + k) % planes
        return peer, {"gx": (peer // ny) * nz + z, "gy": peer % ny}

    def greet_plane(k, c):
        pl.semaphore_signal(barrier, inc=1, device_id=in_plane(k)[1], device_id_type=MESH)
        return c

    reach = nz // 4
    for k in range(1, reach + 1):
        for way in (k, nz - k):
            pl.semaphore_signal(barrier, inc=1, device_id=in_line(way), device_id_type=MESH)
    lax.fori_loop(1, planes, greet_plane, 0)
    sides = [(-1, 0), (1, 0), (0, -1), (0, 1), (-1, -1), (-1, 1), (1, -1), (1, 1)]

    def beside(side):
        return {"gx": (gx + side[0] + nx) % nx, "gy": (gy + side[1] + ny) % ny}

    for side in sides[:2] + sides[4:]:
        pl.semaphore_signal(barrier, inc=1, device_id=beside(side), device_id_type=MESH)

    load_vec = load(basis_in.at[KB - 1], basis.at[KB - 1], 0)
    load_box = load(box_in, box, 1)
    load_up = load(up_in, up, 2)
    load_bloch = load(bloch_in, bloch, 3)
    others = pl.ds(0, KB - 1)
    load_basis = load(basis_in.at[others], basis.at[others], 4)
    load_type = load(type_in, kind, 5)
    load_offsets = load(offsets_in, offsets, 6)
    load_near = load(near_in, near_mats, 7)
    load_top = load(top_in, top, 8)
    load_tmats = load(tmats_in, tmats, 9)

    pending = []

    def send_line(src, dst, sem, rows, scatter):
        def body(k, c):
            far_half = nz // 2 + ((k + 1) // 2) * (1 - 2 * (k % 2))
            peer = (z + far_half) % nz
            pltpu.make_async_remote_copy(
                src.at[peer if scatter else z, pl.ds(0, rows)],
                dst.at[z, pl.ds(0, rows)],
                sem.at[0], sem.at[1], device_id=in_line(far_half), device_id_type=MESH,
            ).start()
            return c

        lax.fori_loop(0, nz - 1, body, 0)
        pending.append((src, sem, nz - 1, rows))

    def send_plane(src, dst, sem, rows, scatter):
        def body(k, c):
            peer, device = in_plane(1 + (k + planes // 2 + ny // 2 - 2) % (planes - 1))
            pltpu.make_async_remote_copy(
                src.at[peer if scatter else spot_in_plane, pl.ds(0, rows)],
                dst.at[spot_in_plane, pl.ds(0, rows)],
                sem.at[0], sem.at[1], device_id=device, device_id_type=MESH,
            ).start()
            return c

        lax.fori_loop(1, planes, body, 0)
        pending.append((src, sem, planes - 1, rows))

    def wait_all(buf, sem, number, rows):
        span = buf.at[pl.ds(0, number), pl.ds(0, rows)]
        pltpu.make_async_copy(span, span, sem).wait()

    load_box.wait()
    boxes = box[...]
    quarters = ((boxes >> 7) & 1) * 2 + ((boxes >> 3) & 1)
    quarter_of = jnp.concatenate(
        [ones_where(iota((16, COEF), 0) == quarters[r : r + 1, :]) for r in range(SD // COEF)], axis=1
    )
    load_up.wait()
    up_high, up_low = split(up[...])
    load_vec.wait()
    vector_pair = jnp.concatenate(split(basis[KB - 1]), axis=1)
    quad2 = dot(quarter_of, vector_pair)
    quad_high, quad_low = split((quad2[:, :COEF] + quad2[:, COEF:])[0:8])
    pair = jnp.concatenate([quad_high.astype(f32), quad_low.astype(f32)], axis=0).astype(bf16)
    raised = dot(pair, up_high) + dot(pair, up_low)
    ebuf[spot_in_plane, 0:4, :] = (raised[0:8] + raised[8:16])[0:4]
    pl.semaphore_wait(barrier, 2 * reach + planes - 1 + 6)
    send_plane(ebuf, ebuf, e_sem, 4, False)
    for i, way in enumerate((reach, nz - reach)):
        pl.semaphore_signal(met.at[i], inc=1, device_id=in_line(way), device_id_type=MESH)

    member = jnp.concatenate(
        [ones_where(iota((BOXES, COEF), 0) == boxes[r : r + 1, :]) for r in range(SD // COEF)], axis=1
    )
    leaf2 = dot(member, vector_pair)
    leaf = (leaf2[:, :COEF] + leaf2[:, COEF:]).reshape(LX, LY, COEF)

    edges[0] = leaf[0]
    edges[1] = leaf[LX - 1]
    edges[2] = leaf[:, 0, :]
    edges[3] = leaf[:, LY - 1, :]
    for c, (x, y) in enumerate([(0, 0), (0, LY - 1), (LX - 1, 0), (LX - 1, LY - 1)]):
        corners[c, 0:1, :] = leaf[x, y : y + 1, :]
    halo = []
    for i, side in enumerate(sides):
        other = sides.index((-side[0], -side[1]))
        if i < 4:
            src, dst = edges.at[i], rim.at[other]
        else:
            src, dst = corners.at[i - 4], rim_corners.at[other - 4]
        copy = pltpu.make_async_remote_copy(
            src, dst, h_send.at[i], h_recv.at[other], device_id=beside(side), device_id_type=MESH
        )
        copy.start()
        halo.append(copy)
    pad[1 : LX + 1, 8 : 8 + LY, :] = leaf

    load_bloch.wait()
    theta = (bloch[0], bloch[1])
    weights = far_weights(nx, ny, nz, gx, gy, theta)
    far_w[0], far_w[1] = split(weights)

    wait_all(ebuf, e_sem.at[1], planes - 1, 4)
    sources = ebuf[...].reshape(8 * planes, COEF)
    turned = pltpu.roll(times_i(sources), 4, 0)
    sources = jnp.where((iota(sources.shape, 0) & 4) == 0, sources, turned)
    source_high, source_low = split(sources)
    part2 = dot(far_w[0], jnp.concatenate([source_high, source_low], axis=1))
    part = part2[:, :COEF] + part2[:, COEF:] + dot(far_w[1], source_high)
    for j in range(nz):
        pbuf[j, 0:4, :] = part[4 * j : 4 * j + 4]
    rbuf[z, 0:4, :] = pbuf[z, 0:4, :]
    for i in range(2):
        pl.semaphore_wait(met.at[i], 1)
    send_line(pbuf, rbuf, r_sem, 4, True)

    load_basis.wait()
    grams = []
    for j in range(KB):
        for k in range(j, KB):
            grams.append(fold(basis[j] * basis[k]))
    gram_lanes = to_lanes(grams, KB + 1)

    load_type.wait()
    codes = boxes + BOXES * kind[...]
    for r in range(SD // COEF):
        code = jnp.broadcast_to(codes[r : r + 1, :], (COEF, COEF)).T
        own_box = code & (BOXES - 1)
        own_type = code >> 8
        lane = iota((COEF, COEF), 1)
        rows = pl.ds(r * COEF, COEF)
        member_t[rows, 0:COEF] = ones_where(own_box == lane)
        member_t[rows, COEF:BOXES] = ones_where(own_box == lane + COEF)
        spot = own_type * 8 + ((own_box >> 7) & 1) * 2 + ((own_box >> 3) & 1)
        hot[rows, :] = ones_where(spot == (lane & 63))
        field[rows, :] = own_type

    spots = kind[...] * 8 + quarters
    hot_t = jnp.concatenate(
        [ones_where(iota((8 * NTYPE, COEF), 0) == spots[r : r + 1, :]) for r in range(SD // COEF)], axis=1
    )
    numbers = jnp.sum(hot_t.astype(f32), axis=1, keepdims=True)

    def class_sums(x):
        both = dot(hot_t, jnp.concatenate(split(x), axis=1))
        return both[:, :COEF] + both[:, COEF:]

    basis_sums = [class_sums(basis[k]) for k in range(KB)]

    load_top.wait()
    load_tmats.wait()
    every = jnp.concatenate([tmats[t] for t in range(NTYPE)], axis=1)
    every_high, every_low = split(every)
    top_high, top_low = split(top[...])
    top_t[0], top_t[1] = split(dot(top_high, every_high) + dot(top_low, every_high) + dot(top_high, every_low))
    every3 = jnp.concatenate([every_high, every_high, every_low], axis=0)

    load_offsets.wait()
    load_near.wait()
    for copy in halo:
        copy.wait_recv()
    crossings = []
    row_cross = {-1: jnp.where(gx == 0, -1.0, 0.0), 0: 0.0, 1: jnp.where(gx == nx - 1, 1.0, 0.0)}
    col_cross = {-1: jnp.where(gy == 0, -1.0, 0.0), 0: 0.0, 1: jnp.where(gy == ny - 1, 1.0, 0.0)}
    angle = jnp.zeros((8, COEF), f32)
    for i, side in enumerate(sides):
        value = row_cross[side[0]] * theta[0] + col_cross[side[1]] * theta[1]
        angle = jnp.where(iota((8, COEF), 0) == i, value, angle)
    cosine, sine = jnp.cos(angle), jnp.sin(angle)

    def rotated(x, i):
        return cosine[i : i + 1] * x + sine[i : i + 1] * times_i(x)

    pad[0, 8 : 8 + LY, :] = rotated(rim[0], 0)
    pad[LX + 1, 8 : 8 + LY, :] = rotated(rim[1], 1)
    west, east = rotated(rim[2], 2), rotated(rim[3], 3)
    for x in range(LX):
        pad[x + 1, 7:8, :] = west[x : x + 1, :]
        pad[x + 1, 8 + LY : 9 + LY, :] = east[x : x + 1, :]
    for c, (x, y) in enumerate([(0, 7), (0, 8 + LY), (LX + 1, 7), (LX + 1, 8 + LY)]):
        pad[x, y : y + 1, :] = rotated(rim_corners[c], 4 + c)

    highs, lows, mats_high, mats_low = [], [], [], []
    for b in (-1, 0, 1):
        shifted = pad[:, 8 + b : 8 + b + LY, :].reshape((LX + 2) * LY, COEF)
        high, low = split(shifted)
        for a in (-1, 0, 1):
            entry = 0
            for o in range(NOFF):
                here = (offsets[0, o] == a) & (offsets[1, o] == b)
                entry = jnp.where(here, o, entry)
            mat_high, mat_low = split(near_mats[entry])
            start = (1 + a) * LY
            highs.append(high[start : start + BOXES])
            lows.append(low[start : start + BOXES])
            mats_high.append(mat_high)
            mats_low.append(mat_low)
    mat_high = jnp.concatenate(mats_high, axis=0)
    mats = jnp.concatenate([mat_high, jnp.concatenate(mats_low, axis=0)], axis=1)
    near2 = dot(jnp.concatenate(highs, axis=1), mats)
    near = near2[:, :COEF] + near2[:, COEF:] + dot(jnp.concatenate(lows, axis=1), mat_high)

    near_pair = jnp.concatenate(split(near), axis=1)
    for r in range(SD // CHUNK):
        rows = pl.ds(r * CHUNK, CHUNK)
        at2 = dot(member_t[rows, :], near_pair)
        at_high, at_low = split(at2[:, :COEF] + at2[:, COEF:])
        all_types = dot(jnp.concatenate([at_high, at_low, at_high], axis=1), every3)
        own_type = field[rows, :]
        value = all_types[:, :COEF]
        for t in range(1, NTYPE):
            value = jnp.where(own_type == t, all_types[:, t * COEF : (t + 1) * COEF], value)
        image[rows, :] = -value

    near_sums = [fold(basis[k] * image[...]) for k in range(KB)] + [fold(image[...] * image[...])]
    near_class = class_sums(image[...])

    wait_all(rbuf, r_sem.at[1], nz - 1, 4)
    arrived = jnp.sum(rbuf[...], axis=0)
    far = jnp.where(iota((8, COEF), 0) < 4, arrived, 0.0)
    far_high, far_low = split(far)
    far_pair = jnp.concatenate([far_high.astype(f32), far_low.astype(f32)], axis=0).astype(bf16)
    table2 = dot(far_pair, top_t[0]) + dot(far_pair, top_t[1])
    table = table2[0:8] + table2[8:16]
    table = jnp.concatenate([table[:, t * COEF : (t + 1) * COEF] for t in range(NTYPE)], axis=0)
    sums = [near_sums[k] - fold(table * basis_sums[k]) for k in range(KB)]
    sums.append(near_sums[KB] + fold(table * (table * numbers - 2.0 * near_class)))

    bbuf[spot_in_plane, 0:1, :] = to_lanes(sums) + gram_lanes
    send_plane(bbuf, bbuf, b_sem, 1, False)
    table = jnp.concatenate(split(table), axis=0)
    for r in range(SD // CHUNK):
        rows = pl.ds(r * CHUNK, CHUNK)
        image[rows, :] = image[rows, :] - dot(hot[rows, :], table)
    wait_all(bbuf, b_sem.at[1], planes - 1, 1)
    abuf[z, 0:1, :] = jnp.sum(bbuf[...], axis=0)
    send_line(abuf, abuf, a_sem, 1, False)
    wait_all(abuf, a_sem.at[1], nz - 1, 1)
    totals = jnp.sum(abuf[...], axis=0)
    inner = [total_lane(totals, k) for k in range(KB)]
    square = total_lane(totals, KB)
    gram, lane = {}, KB + 1
    for j in range(KB):
        for k in range(j, KB):
            gram[j, k] = gram[k, j] = total_lane(totals, lane)
            lane += 1
    coeffs = [(inner[k] + gram[k, KB - 1]) / count for k in range(KB)]
    step = [coeffs[k] - (1.0 if k == KB - 1 else 0.0) for k in range(KB)]
    for k in range(KB):
        along = -2.0 * inner[k]
        for j in range(KB):
            along = along + gram[k, j] * step[j]
        square = square + step[k] * along
    beta = jnp.sqrt(jnp.maximum(square, 0.0) / count + 1e-06)
    scale = 1.0 / beta

    for k, value in enumerate(coeffs + [beta]):
        hess_ref[k] = jnp.sum(value)
    for r in range(SD // CHUNK):
        rows = pl.ds(r * CHUNK, CHUNK)
        w = image[rows, :]
        for k in range(KB):
            w = w - step[k] * basis[k, rows, :]
        out_ref[rows, :] = w * scale
    for copy in halo:
        copy.wait_send()
    for buf, sem, number, rows in pending:
        wait_all(buf, sem.at[0], number, rows)


def on_device(nx, ny, basis, sphere_box, sphere_type, near_offsets, near_mats, up_mat, top_mat, tmats, bloch_angle):
    nz = nx // 2
    vmem, dma = pltpu.VMEM, pltpu.SemaphoreType.DMA
    return pl.pallas_call(
        functools.partial(kernel, nx, ny),
        out_shape=(pltpu.VMEM((SD, COEF), f32), pltpu.SMEM((KB + 1,), f32)),
        in_specs=[pl.BlockSpec(memory_space=pltpu.HBM)] * 9,
        out_specs=(pl.BlockSpec(memory_space=pltpu.VMEM), pl.BlockSpec(memory_space=pltpu.SMEM)),
        scratch_shapes=[
            vmem((KB, SD, COEF), f32),
            vmem((SD // COEF, COEF), i32),
            vmem((SD // COEF, COEF), i32),
            pltpu.SMEM((2, NOFF), i32),
            vmem((NOFF, COEF, COEF), f32),
            vmem((COEF, COEF), f32),
            vmem((COEF, COEF), f32),
            vmem((NTYPE, COEF, COEF), f32),
            pltpu.SMEM((2,), f32),
            vmem((2 * ny, 8, COEF), f32),
            vmem((nz, 8, COEF), f32),
            vmem((nz, 8, COEF), f32),
            vmem((nz, 1, COEF), f32),
            vmem((2 * ny, 1, COEF), f32),
            vmem((4, LX, COEF), f32),
            vmem((4, 1, COEF), f32),
            vmem((4, LX, COEF), f32),
            vmem((4, 1, COEF), f32),
            vmem((LX + 2, LY + 16, COEF), f32),
            vmem((2, 4 * nz, 16 * ny), bf16),
            vmem((2, COEF, NTYPE * COEF), bf16),
            vmem((SD, COEF), bf16),
            vmem((SD, BOXES), bf16),
            vmem((SD, COEF), f32),
            vmem((SD, COEF), i32),
            dma((10,)),
            dma((2,)),
            dma((2,)),
            dma((2,)),
            dma((2,)),
            dma((8,)),
            dma((8,)),
            pltpu.SemaphoreType.REGULAR((2,)),
        ],
        compiler_params=pltpu.CompilerParams(
            collective_id=0, has_side_effects=True, vmem_limit_bytes=48 * 1024 * 1024
        ),
        name="arnoldi_step",
    )(
        *[pltpu.with_memory_space_constraint(x, pltpu.HBM) for x in (basis,
        sphere_box.reshape(SD // COEF, COEF),
        sphere_type.reshape(SD // COEF, COEF),
        near_offsets.T, near_mats, up_mat, top_mat, tmats, bloch_angle)]
    )


def solution(mesh):
    return jax.shard_map(
        functools.partial(on_device, mesh.shape["gx"], mesh.shape["gy"]),
        mesh=mesh,
        in_specs=(
            P(None, ("gx", "gy"), None),
            P(("gx", "gy")),
            P(("gx", "gy")),
            P(),
            P(),
            P(),
            P(),
            P(),
            P(),
        ),
        out_specs=(P(("gx", "gy"), None), P()),
        check_vma=False,
    )
```
